128 devices in a mesh: rng: 8 (over y, x_lo), az: 16 (over x_hi, z, core).
Axes of the slice: x: 4 (x_hi: 2, x_lo: 2; x = x_hi * 2 + x_lo), y: 4, z: 4, core: 2. Of those that a mesh axis runs over, the one named last changes fastest.
Arguments:
- raw_echo: float32 [2, 16384, 4096], P(None, 'az', 'rng'), may hold values from -6 to 6
- chirp_spectrum: float32 [2, 4096], replicated, may hold values from -6 to 6
- azimuth_rate: float32 [4096], P(('rng', 'az')), may hold values from 100 to 400
- shift_table: int32 [16, 4096], P(None, ('rng', 'az')), may hold values from -28 to 29
- filter_index: int32 [16, 4096], P(None, ('rng', 'az')), may hold values from 0 to 15
- tap_table: float32 [16, 8], replicated, may hold values from -3 to 3
Outputs:
- image_out: float32 [2, 4096, 16384], P(None, ('rng', 'az'))
The draws below stay inside these ranges and needn't reach their ends.
All inputs are finite; a program needn't handle non-finite values.
Results may differ from the reference program's by a relative error of at most 0.0003.
Values sent between devices are 32-bit elements; how exact they have to be, the bound alone decides.
A program may use at most 64 MiB of HBM per device.

```python
import math
import jax
import jax.numpy as jnp
from jax import lax

NRG = 4096
NAZ = 16384
GROUPS = 16
NFILT = 16
TAPS = 8
HALO = 32


def touch_ends(result, key, smallest, top_value):
    index_at = [jax.random.randint(jax.random.fold_in(key, axis), (), 0, length) for axis, length in enumerate(result.shape)]
    longest = result.shape.index(max(result.shape))
    next_to = index_at[:longest] + [(index_at[longest] + 1) % result.shape[longest]] + index_at[longest + 1:]
    return result.at[tuple(index_at)].set(smallest).at[tuple(next_to)].set(top_value)


def block_scale(rng, shape, shards, smallest, top_value):
    loudness = 1.0
    for position, shards_of in shards:
        steps = jax.random.uniform(jax.random.fold_in(jax.random.fold_in(rng, 6), position), (shards_of,), jnp.float32, smallest / len(shards), top_value / len(shards))
        loudness = loudness * jnp.repeat(jnp.exp(steps), shape[position] // shards_of).reshape((-1,) + (1,) * (len(shape) - 1 - position))
    return loudness


def scatter_about(key, dims, deviation, reach, cuts=(), held_as=jnp.bfloat16):
    result = jax.random.normal(key, dims, jnp.float32) * deviation
    if len(cuts) > 0:
        result = block_scale(key, dims, cuts, -0.22, 0.18) * result
    return jnp.clip(result, min=-reach, max=reach).astype(held_as)


def setup_inputs(seed: int = 0) -> dict:
    seeds = jax.random.split(jax.random.key(seed), 7)
    return {
        "raw_echo": scatter_about(seeds[0], (2, NAZ, NRG), 1.0, 6.0, ((1, 16), (2, 8)), jnp.float32),
        "chirp_spectrum": scatter_about(seeds[1], (2, NRG), 1.0, 6.0, (), jnp.float32),
        "azimuth_rate": jnp.clip(jnp.exp(math.log(400.0) - 1.3862944 * jax.random.uniform(seeds[2], (NRG,), jnp.float32) ** block_scale(seeds[2], (NRG,), ((0, 128),), -0.2, 0.2)), 100.0, 400.0),
        "shift_table": touch_ends(jax.random.randint(seeds[3], (GROUPS, NRG), 4 - HALO, HALO - 2), jax.random.fold_in(seeds[3], 1), 4 - HALO, (HALO - 2) - 1).astype(jnp.int32),
        "filter_index": touch_ends(jax.random.randint(seeds[4], (GROUPS, NRG), 0, NFILT), jax.random.fold_in(seeds[4], 1), 0, NFILT - 1).astype(jnp.int32),
        "tap_table": scatter_about(seeds[5], (NFILT, TAPS), 0.35, 3.0, (), jnp.float32),
    }


def reference(raw_echo, chirp_spectrum, azimuth_rate, shift_table, filter_index, tap_table):
    echo_data = lax.complex(raw_echo[0], raw_echo[1])
    chirp_ref = lax.complex(chirp_spectrum[0], chirp_spectrum[1])
    compressed = jnp.fft.ifft(jnp.fft.fft(echo_data, axis=1) * chirp_ref[None, :], axis=1)
    doppler = jnp.fft.fft(compressed, axis=0).T
    padded = jnp.pad(doppler, ((HALO, HALO), (0, 0)))
    band_len = NAZ // GROUPS
    weights = tap_table[filter_index]
    bin_ids = jnp.arange(NRG, dtype=jnp.int32)

    def one_band(band_id):
        band_data = lax.dynamic_slice_in_dim(padded, band_id * band_len, band_len, 1)
        band_weights = weights[band_id]
        band_shift = shift_table[band_id]
        summed = jnp.zeros((NRG, band_len), doppler.dtype)
        for tap_id in range(TAPS):
            source = bin_ids + band_shift + (tap_id - 4 + HALO)
            summed = summed + band_weights[:, tap_id][:, None] * band_data[source]
        return summed

    migrated = lax.map(one_band, jnp.arange(GROUPS, dtype=jnp.int32))
    migrated = migrated.transpose(1, 0, 2).reshape(NRG, NAZ)
    freq_ids = jnp.arange(NAZ, dtype=jnp.int32)
    centred = ((freq_ids + NAZ // 2) % NAZ - NAZ // 2).astype(jnp.float32) / NAZ
    phase_map = (jnp.pi * azimuth_rate)[:, None] * (centred * centred)[None, :]
    focused = migrated * lax.complex(jnp.cos(phase_map), -jnp.sin(phase_map))
    image_out = jnp.fft.ifft(focused, axis=1)
    return jnp.stack([jnp.real(image_out), jnp.imag(image_out)]).astype(jnp.float32)
```

```python
import functools

import jax
import jax.numpy as jnp
import ml_dtypes
import numpy as np
from jax import lax
from jax.experimental import pallas as pl
from jax.experimental.pallas import tpu as pltpu
from jax.sharding import PartitionSpec as P

NRG = 4096
NAZ = 16384
GROUPS = 16
NFILT = 16
TAPS = 8
HALO = 32

NR = 8
NA = 16
NDEV = NR * NA
BINS = NRG // NDEV
LINES = NAZ // NDEV
CHUNKS = 4
CL = LINES // CHUNKS
HALVES = 2
HB = BINS // HALVES
HROWS = NDEV * 2 * HB
BLK = 2 * HB
PAIRS = BINS // 2

F32 = jnp.float32
BF16 = jnp.bfloat16
MESH = pl.DeviceIdType.MESH


def dft_matrix(sign):
    ids = np.arange(128)
    ang = 2.0 * np.pi * (np.outer(ids, ids) % 128) / 128
    c, s = np.cos(ang), sign * np.sin(ang)
    return np.block([[c, -s], [s, c]])


def split_matrix(m):
    hi = m.astype(ml_dtypes.bfloat16)
    lo = (m - hi.astype(np.float64)).astype(ml_dtypes.bfloat16)
    return np.concatenate([hi, hi, lo], axis=1)


def tables():
    wf = split_matrix(dft_matrix(-1.0))
    wi = split_matrix(dft_matrix(1.0))
    wft = np.ascontiguousarray(wf.T)
    k0 = np.arange(32)[:, None]
    b = np.arange(128)[None, :]
    ang = 2.0 * np.pi * (k0 * b % NRG) / NRG
    tw = np.stack([np.cos(ang), -np.sin(ang)])
    tw_in = np.repeat(tw[:, :, None, :], 8, axis=2).astype(np.float32)
    tw_out = np.stack([np.cos(ang), np.sin(ang)])
    tw_out = np.repeat(tw_out.transpose(1, 0, 2)[..., None], 128, axis=3).astype(np.float32)
    ids = np.arange(128)
    ang = 2.0 * np.pi * np.outer(ids, ids) / NAZ
    tw_az = np.stack([np.cos(ang), -np.sin(ang)]).astype(np.float32)
    return wf, wi, wft, tw_in, tw_out, tw_az


def cadd(x, y):
    return (x[0] + y[0], x[1] + y[1])


def csub(x, y):
    return (x[0] - y[0], x[1] - y[1])


def cmul_i(x, sign):
    if sign > 0:
        return (-x[1], x[0])
    return (x[1], -x[0])


def cmul_const(x, num, den, sign):
    num = num % den
    if num == 0:
        return x
    ang = 2.0 * np.pi * num / den
    c, s = float(np.cos(ang)), float(sign * np.sin(ang))
    return (x[0] * c - x[1] * s, x[0] * s + x[1] * c)


def dft4(x, sign):
    a, b = cadd(x[0], x[2]), csub(x[0], x[2])
    c, d = cadd(x[1], x[3]), cmul_i(csub(x[1], x[3]), sign)
    return [cadd(a, c), cadd(b, d), csub(a, c), csub(b, d)]


def dft8(x, sign):
    even = dft4([x[0], x[2], x[4], x[6]], sign)
    odd = dft4([x[1], x[3], x[5], x[7]], sign)
    h = float(np.sqrt(0.5))
    o1 = odd[1]
    o3 = odd[3]
    if sign > 0:
        t1 = ((o1[0] - o1[1]) * h, (o1[0] + o1[1]) * h)
        t3 = ((-o3[0] - o3[1]) * h, (o3[0] - o3[1]) * h)
    else:
        t1 = ((o1[0] + o1[1]) * h, (o1[1] - o1[0]) * h)
        t3 = ((o3[1] - o3[0]) * h, (-o3[0] - o3[1]) * h)
    t = [odd[0], t1, cmul_i(odd[2], sign), t3]
    return [cadd(even[k], t[k]) for k in range(4)] + [csub(even[k], t[k]) for k in range(4)]


def dft32(load, sign):
    cols = []
    for a in range(4):
        y = dft8([load(4 * s + a) for s in range(8)], sign)
        cols.append([cmul_const(y[k], a * k, 32, sign) for k in range(8)])
    out = [None] * 32
    for k in range(8):
        z = dft4([cols[a][k] for a in range(4)], sign)
        for m in range(4):
            out[k + 8 * m] = z[m]
    return out


def three(x, axis):
    hi = x.astype(BF16)
    lo = (x - hi.astype(F32)).astype(BF16)
    return jnp.concatenate([hi, lo, hi], axis=axis)


def dot_nn(a, b):
    return lax.dot_general(a, b, (((1,), (0,)), ((), ())), preferred_element_type=F32)


def dot_nt(a, b):
    return lax.dot_general(a, b, (((1,), (1,)), ((), ())), preferred_element_type=F32)


def dft_pair(w_ref, x, tw_ref, conj):
    y = dot_nn(w_ref[...], three(x, 0))
    tr, ti = tw_ref[0], tw_ref[1]
    if conj:
        ti = -ti
    rows = []
    for m in range(2):
        yr = y[:128, 128 * m : 128 * m + 128]
        yi = y[128:, 128 * m : 128 * m + 128]
        rows.append(jnp.concatenate([yr * tr - yi * ti, yr * ti + yi * tr], axis=1))
    return dot_nt(w_ref[...], three(jnp.concatenate(rows, axis=0), 1))


def half_turns(theta):
    m = jnp.floor(theta + 0.5)
    d = theta - m
    half = m * 0.5
    sign = 1.0 - 4.0 * (half - jnp.floor(half))
    x = d * d
    pi = np.pi
    cs = [float((-1) ** n * pi ** (2 * n) / np.prod(np.arange(1.0, 2 * n + 1))) for n in range(7)]
    sn = [
        float((-1) ** n * pi ** (2 * n + 1) / np.prod(np.arange(1.0, 2 * n + 2))) for n in range(6)
    ]
    c = cs[6]
    for n in range(5, -1, -1):
        c = c * x + cs[n]
    s = sn[5]
    for n in range(4, -1, -1):
        s = s * x + sn[n]
    return c * sign, s * d * sign


def kernel(
    raw, chirp, tw_out_hbm, wf, wi, wft, tw_in, tw_az, rate, shift, filt, taps,
    out,
    xb, ub, cb, db, fb, pb, twb, ob, mb, c2b,
    sem_tw, send1, recv1, send2, recv2, sendh, recvh, sem_out,
):
    i = lax.axis_index("rng")
    j = lax.axis_index("az")
    r = i * NA + j
    q = j * NR + i

    def device(block):
        return (lax.div(block, NA), lax.rem(block, NA))

    barrier = pltpu.get_barrier_semaphore()

    def greet(k, _):
        pl.semaphore_signal(
            barrier, inc=1, device_id=device(lax.rem(r + k, NDEV)), device_id_type=MESH
        )
        return 0

    lax.fori_loop(1, NDEV, greet, 0)
    pl.semaphore_wait(barrier, NDEV - 1)

    for ch in range(CHUNKS):

        def lines(block, ch=ch):
            return pl.ds(pl.multiple_of(block * LINES + ch * CL, CL), CL)

        def send_lines(k, _, ch=ch, lines=lines):
            to = lax.rem(i + k, NR)
            pltpu.make_async_remote_copy(
                src_ref=raw.at[:, lines(to), :],
                dst_ref=xb.at[i, :, pl.ds(ch * CL, CL), :],
                send_sem=send1.at[ch],
                recv_sem=recv1.at[ch],
                device_id=(to, j),
                device_id_type=MESH,
            ).start()
            return 0

        lax.fori_loop(1, NR, send_lines, 0)
        pltpu.make_async_copy(
            raw.at[:, lines(i), :], xb.at[i, :, pl.ds(ch * CL, CL), :], recv1.at[ch]
        ).start()

    tw_copy = pltpu.make_async_copy(tw_out_hbm, twb, sem_tw)
    tw_copy.start()

    f1 = lax.broadcasted_iota(jnp.int32, (128, 128), 0)
    f0 = lax.broadcasted_iota(jnp.int32, (128, 128), 1)
    freq = f0 + 128 * f1
    freq = jnp.where(freq >= NAZ // 2, freq - NAZ, freq)
    c = freq.astype(F32) * (1.0 / NAZ)
    c2b[...] = c * c

    def phases(b, _):
        cosine, sine = half_turns(rate[b] * c2b[...])
        pb[b, 0] = cosine * (1.0 / NAZ)
        pb[b, 1] = sine * (1.0 / NAZ)
        return 0

    lax.fori_loop(0, BINS, phases, 0)

    for ch in range(CHUNKS):
        chunk = xb.at[:, :, pl.ds(ch * CL, CL), :]
        pltpu.make_async_copy(chunk, chunk, recv1.at[ch]).wait()

        def first(t, _, ch=ch):
            rows = pl.ds(pl.multiple_of(ch * CL + t * 8, 8), 8)

            def load(n):
                lanes = pl.ds(128 * (n % 4), 128)
                return (xb[n // 4, 0, rows, lanes], xb[n // 4, 1, rows, lanes])

            res = dft32(load, -1.0)
            for k in range(32):
                lanes = pl.ds(128 * (k % 4), 128)
                tr, ti = tw_in[0, k], tw_in[1, k]
                xr, xi = res[k]
                xb[k // 4, 0, rows, lanes] = xr * tr - xi * ti
                xb[k // 4, 1, rows, lanes] = xr * ti + xi * tr
            return 0

        lax.fori_loop(0, CL // 8, first, 0)

        def second(blk, _, ch=ch):
            rows = pl.ds(ch * CL, CL)
            parts = []
            for m in range(8):
                s = blk * 2 + m // 4
                lanes = pl.ds(128 * (m % 4), 128)
                parts.append(
                    jnp.concatenate([xb[s, 0, rows, lanes], xb[s, 1, rows, lanes]], axis=1)
                )
            y = dot_nn(three(jnp.concatenate(parts, axis=0), 1), wft[...])
            for m in range(8):
                s = blk * 2 + m // 4
                lanes = pl.ds(128 * (m % 4), 128)
                yr = y[m * CL : m * CL + CL, :128]
                yi = y[m * CL : m * CL + CL, 128:]
                hr = chirp[0, pl.ds(blk * 8 + m, 1), :]
                hi = chirp[1, pl.ds(blk * 8 + m, 1), :]
                xb[s, 0, rows, lanes] = yr * hr - yi * hi
                xb[s, 1, rows, lanes] = yr * hi + yi * hr
            return 0

        lax.fori_loop(0, 4, second, 0)

    tw_copy.wait()

    def third(s, _):
        for h in range(2):
            parts = []
            for m in range(2):
                lanes = pl.ds(128 * (2 * h + m), 128)
                parts.append(jnp.concatenate([xb[s, 0, :, lanes], xb[s, 1, :, lanes]], axis=1))
            y = dot_nt(wi[...], three(jnp.concatenate(parts, axis=0), 1))
            for m in range(2):
                k = s * 4 + 2 * h + m
                yr = y[:128, 128 * m : 128 * m + 128]
                yi = y[128:, 128 * m : 128 * m + 128]
                tr, ti = twb[k, 0], twb[k, 1]
                ub[k, 0] = yr * tr - yi * ti
                ub[k, 1] = yr * ti + yi * tr
        return 0

    lax.fori_loop(0, NR, third, 0)

    def make_block(n, _):
        half = lax.div(n, 4)
        beta = lax.rem(n, 4)

        def fourth(t, _):
            rows = pl.ds(pl.multiple_of(32 * beta + HB * half + 8 * t, 8), 8)

            def load(k):
                return (ub[k, 0, rows, :], ub[k, 1, rows, :])

            res = dft32(load, 1.0)
            for a in range(32):
                base = half * HROWS + (4 * a + beta) * BLK + 8 * t
                cb[pl.ds(pl.multiple_of(base, 8), 8), :] = res[a][0]
                cb[pl.ds(pl.multiple_of(base + HB, 8), 8), :] = res[a][1]
            return 0

        lax.fori_loop(0, HB // 8, fourth, 0)
        mine = pl.ds(pl.multiple_of(half * HROWS + q * BLK, 8), BLK)

        def send_block(k, _):
            to = 4 * lax.rem(lax.div(r, 4) + k, 32) + beta
            theirs = pl.ds(pl.multiple_of(half * HROWS + to * BLK, 8), BLK)

            @pl.when(to != r)
            def _():
                pltpu.make_async_remote_copy(
                    src_ref=cb.at[theirs, :],
                    dst_ref=db.at[mine, :],
                    send_sem=send2.at[half],
                    recv_sem=recv2.at[half],
                    device_id=device(to),
                    device_id_type=MESH,
                ).start()

            @pl.when(to == r)
            def _():
                pltpu.make_async_copy(cb.at[theirs, :], db.at[mine, :], recv2.at[half]).start()

            return 0

        lax.fori_loop(0, 32, send_block, 0)
        return 0

    lax.fori_loop(0, 4 * HALVES, make_block, 0)

    up = device(lax.rem(r + 1, NDEV))
    down = device(lax.rem(r + NDEV - 1, NDEV))
    for half in range(HALVES):
        landed = db.at[pl.ds(half * HROWS, HROWS), :]
        pltpu.make_async_copy(landed, landed, recv2.at[half]).wait()

        def azimuth(n, _, half=half):
            base = half * HROWS + 2 * n
            cols = []
            for m in range(2):
                re = db[pl.ds(base + m, 128, stride=BLK), :]
                im = db[pl.ds(base + m + HB, 128, stride=BLK), :]
                cols.append(jnp.concatenate([re, im], axis=0))
            y = dft_pair(wf, jnp.concatenate(cols, axis=1), tw_az, False)
            row = half * HB + 2 * n
            fb[BINS + row] = y[:, :128]
            fb[BINS + row + 1] = y[:, 128:]
            own = fb.at[pl.ds(BINS + row, 2)]
            for place, to, d in ((0, up, 0), (2 * BINS, down, 1)):
                pltpu.make_async_remote_copy(
                    src_ref=own,
                    dst_ref=fb.at[pl.ds(place + row, 2)],
                    send_sem=sendh.at[d],
                    recv_sem=recvh.at[d],
                    device_id=to,
                    device_id_type=MESH,
                ).start()
            return 0

        lax.fori_loop(0, HB // 2, azimuth, 0)

    for d, place in ((0, 0), (1, 2 * BINS)):
        landed = fb.at[pl.ds(place, BINS)]
        pltpu.make_async_copy(landed, landed, recvh.at[d]).wait()

    @pl.when(r == 0)
    def _():
        def clear(n, _):
            fb[n] = jnp.zeros((256, 128), F32)
            return 0

        lax.fori_loop(0, BINS, clear, 0)

    @pl.when(r == NDEV - 1)
    def _():
        def clear(n, _):
            fb[2 * BINS + n] = jnp.zeros((256, 128), F32)
            return 0

        lax.fori_loop(0, BINS, clear, 0)

    def focus(n, _):
        for m in range(2):
            b = 2 * n + m
            lanes = pl.ds(128 * m, 128)
            for g in range(GROUPS):
                first_row = BINS + b + shift[g, b] - 4
                which = filt[g, b]
                re, im = pl.ds(8 * g, 8), pl.ds(128 + 8 * g, 8)
                sr = si = None
                for t in range(TAPS):
                    w = taps[which, t]
                    vr = fb[first_row + t, re, :] * w
                    vi = fb[first_row + t, im, :] * w
                    sr = vr if sr is None else sr + vr
                    si = vi if si is None else si + vi
                pc, ps = pb[b, 0, re, :], pb[b, 1, re, :]
                mb[re, lanes] = sr * pc + si * ps
                mb[im, lanes] = si * pc - sr * ps
        y = dft_pair(wi, mb[...], tw_az, True)
        for m in range(2):
            b = 2 * n + m
            for c in range(2):
                base = (c * 4 + lax.div(b, 8)) * 1024 + lax.rem(b, 8)
                ob[pl.ds(base, 128, stride=8), :] = y[128 * c : 128 * c + 128, 128 * m : 128 * m + 128]
        return 0

    outs = []
    for t in range(4):
        lax.fori_loop(4 * t, 4 * t + 4, focus, 0)
        for c in range(2):
            rows = pl.ds((c * 4 + t) * 1024, 1024)
            copy = pltpu.make_async_copy(ob.at[rows, :], out.at[rows, :], sem_out.at[2 * t + c])
            copy.start()
            outs.append(copy)

    for ch in range(CHUNKS):
        gone = xb.at[pl.ds(0, NR - 1), :, pl.ds(ch * CL, CL), :]
        pltpu.make_async_copy(gone, gone, send1.at[ch]).wait()
    for half in range(HALVES):
        gone = cb.at[pl.ds(0, (NDEV - 1) * BLK), :]
        pltpu.make_async_copy(gone, gone, send2.at[half]).wait()
    for d in range(2):
        gone = fb.at[pl.ds(0, BINS)]
        pltpu.make_async_copy(gone, gone, sendh.at[d]).wait()
    for copy in outs:
        copy.wait()


def local(raw_echo, chirp_spectrum, azimuth_rate, shift_table, filter_index, tap_table):
    wf, wi, wft, tw_in, tw_out, tw_az = tables()
    chirp = chirp_spectrum.reshape(2, 128, 32).transpose(0, 2, 1) * (1.0 / NRG)
    vmem = pl.BlockSpec(memory_space=pltpu.VMEM)
    smem = pl.BlockSpec(memory_space=pltpu.SMEM)
    hbm = pl.BlockSpec(memory_space=pl.ANY)
    dma = pltpu.SemaphoreType.DMA
    image = pl.pallas_call(
        kernel,
        out_shape=jax.ShapeDtypeStruct((8192, 128), F32),
        in_specs=[hbm, vmem, hbm, vmem, vmem, vmem, vmem, vmem, smem, smem, smem, smem],
        out_specs=hbm,
        scratch_shapes=[
            pltpu.VMEM((NR, 2, LINES, 512), F32),
            pltpu.VMEM((32, 2, 128, 128), F32),
            pltpu.VMEM((HALVES * HROWS, 128), F32),
            pltpu.VMEM((HALVES * HROWS, 128), F32),
            pltpu.VMEM((3 * BINS, 256, 128), F32),
            pltpu.VMEM((BINS, 2, 128, 128), F32),
            pltpu.VMEM((32, 2, 128, 128), F32),
            pltpu.VMEM((8192, 128), F32),
            pltpu.VMEM((256, 256), F32),
            pltpu.VMEM((128, 128), F32),
            dma,
            dma((CHUNKS,)),
            dma((CHUNKS,)),
            dma((HALVES,)),
            dma((HALVES,)),
            dma((2,)),
            dma((2,)),
            dma((8,)),
        ],
        compiler_params=pltpu.CompilerParams(
            collective_id=0, has_side_effects=True, vmem_limit_bytes=60 * 1024 * 1024
        ),
        cost_estimate=pl.CostEstimate(
            flops=10_000_000_000, bytes_accessed=16 * 1024 * 1024, transcendentals=0
        ),
        name="focus_slab",
    )(
        raw_echo, chirp, tw_out, wf, wi, wft, tw_in, tw_az,
        azimuth_rate, shift_table, filter_index, tap_table,
    )
    image = image.reshape(2, 4, 128, 8, 128).transpose(0, 1, 3, 2, 4)
    return image.reshape(2, BINS, NAZ)


def solution(mesh):
    return jax.shard_map(
        local,
        mesh=mesh,
        in_specs=(
            P(None, "az", "rng"),
            P(),
            P(("rng", "az")),
            P(None, ("rng", "az")),
            P(None, ("rng", "az")),
            P(),
        ),
        out_specs=P(None, ("rng", "az"), None),
        check_vma=False,
    )
```

```python
import functools

import jax
import jax.numpy as jnp
import ml_dtypes
import numpy as np
from jax import lax
from jax.experimental import pallas as pl
from jax.experimental.pallas import tpu as pltpu
from jax.sharding import PartitionSpec as P

NRG = 4096
NAZ = 16384
GROUPS = 16
NFILT = 16
TAPS = 8
HALO = 32

NR = 8
NA = 16
NDEV = NR * NA
BINS = NRG // NDEV
LINES = NAZ // NDEV
CHUNKS = 4
CL = LINES // CHUNKS
HALVES = 2
HB = BINS // HALVES
HROWS = NDEV * 2 * HB
BLK = 2 * HB
PAIRS = BINS // 2

F32 = jnp.float32
BF16 = jnp.bfloat16
MESH = pl.DeviceIdType.MESH


def dft_matrix(sign):
    ids = np.arange(128)
    ang = 2.0 * np.pi * (np.outer(ids, ids) % 128) / 128
    c, s = np.cos(ang), sign * np.sin(ang)
    return np.block([[c, -s], [s, c]])


def split_matrix(m):
    hi = m.astype(ml_dtypes.bfloat16)
    lo = (m - hi.astype(np.float64)).astype(ml_dtypes.bfloat16)
    return np.concatenate([hi, hi, lo], axis=1)


def tables():
    wf = split_matrix(dft_matrix(-1.0))
    wi = split_matrix(dft_matrix(1.0))
    wft = np.ascontiguousarray(wf.T)
    k0 = np.arange(32)[:, None]
    b = np.arange(128)[None, :]
    ang = 2.0 * np.pi * (k0 * b % NRG) / NRG
    tw = np.stack([np.cos(ang), -np.sin(ang)])
    tw_in = np.repeat(tw[:, :, None, :], 8, axis=2).astype(np.float32)
    tw_out = np.stack([np.cos(ang), np.sin(ang)])
    tw_out = np.repeat(tw_out.transpose(1, 0, 2)[..., None], 128, axis=3).astype(np.float32)
    ids = np.arange(128)
    ang = 2.0 * np.pi * np.outer(ids, ids) / NAZ
    tw_az = np.stack([np.cos(ang), -np.sin(ang)]).astype(np.float32)
    return wf, wi, wft, tw_in, tw_out, tw_az


def cadd(x, y):
    return (x[0] + y[0], x[1] + y[1])


def csub(x, y):
    return (x[0] - y[0], x[1] - y[1])


def cmul_i(x, sign):
    if sign > 0:
        return (-x[1], x[0])
    return (x[1], -x[0])


def cmul_const(x, num, den, sign):
    num = num % den
    if num == 0:
        return x
    ang = 2.0 * np.pi * num / den
    c, s = float(np.cos(ang)), float(sign * np.sin(ang))
    return (x[0] * c - x[1] * s, x[0] * s + x[1] * c)


def dft4(x, sign):
    a, b = cadd(x[0], x[2]), csub(x[0], x[2])
    c, d = cadd(x[1], x[3]), cmul_i(csub(x[1], x[3]), sign)
    return [cadd(a, c), cadd(b, d), csub(a, c), csub(b, d)]


def dft8(x, sign):
    even = dft4([x[0], x[2], x[4], x[6]], sign)
    odd = dft4([x[1], x[3], x[5], x[7]], sign)
    h = float(np.sqrt(0.5))
    o1 = odd[1]
    o3 = odd[3]
    if sign > 0:
        t1 = ((o1[0] - o1[1]) * h, (o1[0] + o1[1]) * h)
        t3 = ((-o3[0] - o3[1]) * h, (o3[0] - o3[1]) * h)
    else:
        t1 = ((o1[0] + o1[1]) * h, (o1[1] - o1[0]) * h)
        t3 = ((o3[1] - o3[0]) * h, (-o3[0] - o3[1]) * h)
    t = [odd[0], t1, cmul_i(odd[2], sign), t3]
    return [cadd(even[k], t[k]) for k in range(4)] + [csub(even[k], t[k]) for k in range(4)]


def dft32(load, sign):
    cols = []
    for a in range(4):
        y = dft8([load(4 * s + a) for s in range(8)], sign)
        cols.append([cmul_const(y[k], a * k, 32, sign) for k in range(8)])
    out = [None] * 32
    for k in range(8):
        z = dft4([cols[a][k] for a in range(4)], sign)
        for m in range(4):
            out[k + 8 * m] = z[m]
    return out


def three(x, axis):
    hi = x.astype(BF16)
    lo = (x - hi.astype(F32)).astype(BF16)
    return jnp.concatenate([hi, lo, hi], axis=axis)


def dot_nn(a, b):
    return lax.dot_general(a, b, (((1,), (0,)), ((), ())), preferred_element_type=F32)


def dot_nt(a, b):
    return lax.dot_general(a, b, (((1,), (1,)), ((), ())), preferred_element_type=F32)


def dft_pair(w_ref, x, tw_ref, conj):
    y = dot_nn(w_ref[...], three(x, 0))
    tr, ti = tw_ref[0], tw_ref[1]
    if conj:
        ti = -ti
    rows = []
    for m in range(2):
        yr = y[:128, 128 * m : 128 * m + 128]
        yi = y[128:, 128 * m : 128 * m + 128]
        rows.append(jnp.concatenate([yr * tr - yi * ti, yr * ti + yi * tr], axis=1))
    return dot_nt(w_ref[...], three(jnp.concatenate(rows, axis=0), 1))


def half_turns(theta):
    m = jnp.floor(theta + 0.5)
    d = theta - m
    half = m * 0.5
    sign = 1.0 - 4.0 * (half - jnp.floor(half))
    x = d * d
    pi = np.pi
    cs = [float((-1) ** n * pi ** (2 * n) / np.prod(np.arange(1.0, 2 * n + 1))) for n in range(7)]
    sn = [
        float((-1) ** n * pi ** (2 * n + 1) / np.prod(np.arange(1.0, 2 * n + 2))) for n in range(6)
    ]
    c = cs[6]
    for n in range(5, -1, -1):
        c = c * x + cs[n]
    s = sn[5]
    for n in range(4, -1, -1):
        s = s * x + sn[n]
    return c * sign, s * d * sign


def kernel(
    raw, chirp, tw_out_hbm, wf, wi, wft, tw_in, tw_az, rate, shift, filt, taps,
    out,
    xb, ub, cb, db, fb, pb, twb, mb, c2b,
    sem_tw, send1, recv1, send2, recv2, sendh, recvh, sem_out,
):
    i = lax.axis_index("rng")
    j = lax.axis_index("az")
    r = i * NA + j
    q = j * NR + i

    def device(block):
        return (lax.div(block, NA), lax.rem(block, NA))

    barrier = pltpu.get_barrier_semaphore()

    def greet(k, _):
        pl.semaphore_signal(
            barrier, inc=1, device_id=device(lax.rem(r + k, NDEV)), device_id_type=MESH
        )
        return 0

    lax.fori_loop(1, NDEV, greet, 0)
    pl.semaphore_wait(barrier, NDEV - 1)

    for ch in range(CHUNKS):

        def lines(block, ch=ch):
            return pl.ds(pl.multiple_of(block * LINES + ch * CL, CL), CL)

        def send_lines(k, _, ch=ch, lines=lines):
            to = lax.rem(i + k, NR)
            pltpu.make_async_remote_copy(
                src_ref=raw.at[:, lines(to), :],
                dst_ref=xb.at[i, :, pl.ds(ch * CL, CL), :],
                send_sem=send1.at[ch],
                recv_sem=recv1.at[ch],
                device_id=(to, j),
                device_id_type=MESH,
            ).start()
            return 0

        lax.fori_loop(1, NR, send_lines, 0)
        pltpu.make_async_copy(
            raw.at[:, lines(i), :], xb.at[i, :, pl.ds(ch * CL, CL), :], recv1.at[ch]
        ).start()

    tw_copy = pltpu.make_async_copy(tw_out_hbm, twb, sem_tw)
    tw_copy.start()

    f1 = lax.broadcasted_iota(jnp.int32, (128, 128), 0)
    f0 = lax.broadcasted_iota(jnp.int32, (128, 128), 1)
    freq = f0 + 128 * f1
    freq = jnp.where(freq >= NAZ // 2, freq - NAZ, freq)
    c = freq.astype(F32) * (1.0 / NAZ)
    c2b[...] = c * c

    def phases(b, _):
        cosine, sine = half_turns(rate[b] * c2b[...])
        pb[b, 0] = cosine * (1.0 / NAZ)
        pb[b, 1] = sine * (1.0 / NAZ)
        return 0

    lax.fori_loop(0, BINS, phases, 0)

    for ch in range(CHUNKS):
        chunk = xb.at[:, :, pl.ds(ch * CL, CL), :]
        pltpu.make_async_copy(chunk, chunk, recv1.at[ch]).wait()

        def first(t, _, ch=ch):
            rows = pl.ds(pl.multiple_of(ch * CL + t * 8, 8), 8)

            def load(n):
                lanes = pl.ds(128 * (n % 4), 128)
                return (xb[n // 4, 0, rows, lanes], xb[n // 4, 1, rows, lanes])

            res = dft32(load, -1.0)
            for k in range(32):
                lanes = pl.ds(128 * (k % 4), 128)
                tr, ti = tw_in[0, k], tw_in[1, k]
                xr, xi = res[k]
                xb[k // 4, 0, rows, lanes] = xr * tr - xi * ti
                xb[k // 4, 1, rows, lanes] = xr * ti + xi * tr
            return 0

        lax.fori_loop(0, CL // 8, first, 0)

        def second(blk, _, ch=ch):
            rows = pl.ds(ch * CL, CL)
            parts = []
            for m in range(8):
                s = blk * 2 + m // 4
                lanes = pl.ds(128 * (m % 4), 128)
                parts.append(
                    jnp.concatenate([xb[s, 0, rows, lanes], xb[s, 1, rows, lanes]], axis=1)
                )
            y = dot_nn(three(jnp.concatenate(parts, axis=0), 1), wft[...])
            for m in range(8):
                s = blk * 2 + m // 4
                lanes = pl.ds(128 * (m % 4), 128)
                yr = y[m * CL : m * CL + CL, :128]
                yi = y[m * CL : m * CL + CL, 128:]
                hr = chirp[0, pl.ds(blk * 8 + m, 1), :]
                hi = chirp[1, pl.ds(blk * 8 + m, 1), :]
                xb[s, 0, rows, lanes] = yr * hr - yi * hi
                xb[s, 1, rows, lanes] = yr * hi + yi * hr
            return 0

        lax.fori_loop(0, 4, second, 0)

    tw_copy.wait()

    def third(s, _):
        for h in range(2):
            parts = []
            for m in range(2):
                lanes = pl.ds(128 * (2 * h + m), 128)
                parts.append(jnp.concatenate([xb[s, 0, :, lanes], xb[s, 1, :, lanes]], axis=1))
            y = dot_nt(wi[...], three(jnp.concatenate(parts, axis=0), 1))
            for m in range(2):
                k = s * 4 + 2 * h + m
                yr = y[:128, 128 * m : 128 * m + 128]
                yi = y[128:, 128 * m : 128 * m + 128]
                tr, ti = twb[k, 0], twb[k, 1]
                row = pl.multiple_of(256 * k, 256)
                ub[pl.ds(row, 128), :] = yr * tr - yi * ti
                ub[pl.ds(row + 128, 128), :] = yr * ti + yi * tr
        return 0

    lax.fori_loop(0, NR, third, 0)

    def shifted(k):
        zh = lax.rem(lax.div(r, 4) + k + lax.div(k, 16), 2)
        x = 2 * lax.rem(lax.div(r, 8), 2) + lax.rem(lax.div(r, 16), 2)
        x = lax.rem(x + k, 4)
        y = lax.rem(lax.div(r, 32) + k + lax.div(k, 4), 4)
        return 8 * y + 4 * lax.rem(x, 2) + 2 * lax.div(x, 2) + zh

    def make_block(n, _):
        half = lax.div(n, 4)
        beta = (lax.rem(n, 4) + lax.rem(r, 4)) - 2 * (
            lax.rem(n, 2) * lax.rem(r, 2) + 2 * lax.rem(lax.div(n, 2), 2) * lax.rem(lax.div(r, 2), 2)
        )

        def fourth(t, _):
            row = pl.multiple_of(32 * beta + HB * half + 8 * t, 8)

            def load(k):
                return (ub[pl.ds(row + 256 * k, 8), :], ub[pl.ds(row + 256 * k + 128, 8), :])

            res = dft32(load, 1.0)
            for a in range(32):
                base = half * HROWS + (4 * a + beta) * BLK + 8 * t
                cb[pl.ds(pl.multiple_of(base, 8), 8), :] = res[a][0]
                cb[pl.ds(pl.multiple_of(base + HB, 8), 8), :] = res[a][1]
            return 0

        lax.fori_loop(0, HB // 8, fourth, 0)
        mine = pl.ds(pl.multiple_of(half * HROWS + q * BLK, 8), BLK)

        def send_block(k, _):
            to = 4 * shifted(k) + beta
            theirs = pl.ds(pl.multiple_of(half * HROWS + to * BLK, 8), BLK)

            @pl.when(to != r)
            def _():
                pltpu.make_async_remote_copy(
                    src_ref=cb.at[theirs, :],
                    dst_ref=db.at[mine, :],
                    send_sem=send2.at[half],
                    recv_sem=recv2.at[half],
                    device_id=device(to),
                    device_id_type=MESH,
                ).start()

            @pl.when(to == r)
            def _():
                pltpu.make_async_copy(cb.at[theirs, :], db.at[mine, :], recv2.at[half]).start()

            return 0

        lax.fori_loop(0, 32, send_block, 0)
        return 0

    lax.fori_loop(0, 4 * HALVES, make_block, 0)

    up = device(lax.rem(r + 1, NDEV))
    down = device(lax.rem(r + NDEV - 1, NDEV))

    def send_halo(row):
        own = fb.at[pl.ds(BINS + row, 4)]
        for place, to, d in ((0, up, 0), (2 * BINS, down, 1)):
            pltpu.make_async_remote_copy(
                src_ref=own,
                dst_ref=fb.at[pl.ds(place + row, 4)],
                send_sem=sendh.at[d],
                recv_sem=recvh.at[d],
                device_id=to,
                device_id_type=MESH,
            ).start()

    for half in range(HALVES):
        landed = db.at[pl.ds(half * HROWS, HROWS), :]
        pltpu.make_async_copy(landed, landed, recv2.at[half]).wait()
        if half == 1:
            for z in range(4):
                send_halo(4 * z)

        def azimuth(n, half=half):
            base = half * HROWS + 2 * n
            cols = []
            for m in range(2):
                re = db[pl.ds(base + m, 128, stride=BLK), :]
                im = db[pl.ds(base + m + HB, 128, stride=BLK), :]
                cols.append(jnp.concatenate([re, im], axis=0))
            y = dft_pair(wf, jnp.concatenate(cols, axis=1), tw_az, False)
            row = half * HB + 2 * n
            fb[BINS + row] = y[:, :128]
            fb[BINS + row + 1] = y[:, 128:]

        def azimuth_two(n, _, half=half, azimuth=azimuth):
            azimuth(2 * n)
            azimuth(2 * n + 1)
            if half == 1:
                send_halo(half * HB + 4 * n)
            return 0

        lax.fori_loop(0, HB // 4, azimuth_two, 0)

    for d, place in ((0, 0), (1, 2 * BINS)):
        landed = fb.at[pl.ds(place, BINS)]
        pltpu.make_async_copy(landed, landed, recvh.at[d]).wait()

    @pl.when(r == 0)
    def _():
        def clear(n, _):
            fb[n] = jnp.zeros((256, 128), F32)
            return 0

        lax.fori_loop(0, BINS, clear, 0)

    @pl.when(r == NDEV - 1)
    def _():
        def clear(n, _):
            fb[2 * BINS + n] = jnp.zeros((256, 128), F32)
            return 0

        lax.fori_loop(0, BINS, clear, 0)

    def focus(n, mb):
        for m in range(2):
            b = 2 * n + m
            lanes = pl.ds(128 * m, 128)
            for g in range(GROUPS):
                first_row = BINS + b + shift[g, b] - 4
                which = filt[g, b]
                re, im = pl.ds(8 * g, 8), pl.ds(128 + 8 * g, 8)
                sr = si = None
                for t in range(TAPS):
                    w = taps[which, t]
                    vr = fb[first_row + t, re, :] * w
                    vi = fb[first_row + t, im, :] * w
                    sr = vr if sr is None else sr + vr
                    si = vi if si is None else si + vi
                pc, ps = pb[b, 0, re, :], pb[b, 1, re, :]
                mb[re, lanes] = sr * pc + si * ps
                mb[im, lanes] = si * pc - sr * ps
        y = dft_pair(wi, mb[...], tw_az, True)
        for m in range(2):
            b = 2 * n + m
            for c in range(2):
                base = (c * 4 + lax.div(b, 8)) * 1024 + lax.rem(b, 8)
                ub[pl.ds(base, 128, stride=8), :] = y[128 * c : 128 * c + 128, 128 * m : 128 * m + 128]

    def focus_two(n, _):
        focus(2 * n, mb.at[0])
        focus(2 * n + 1, mb.at[1])
        return 0

    outs = []
    for t in range(4):
        lax.fori_loop(2 * t, 2 * t + 2, focus_two, 0)
        for c in range(2):
            rows = pl.ds((c * 4 + t) * 1024, 1024)
            copy = pltpu.make_async_copy(ub.at[rows, :], out.at[rows, :], sem_out.at[2 * t + c])
            copy.start()
            outs.append(copy)

    for ch in range(CHUNKS):
        gone = xb.at[pl.ds(0, NR - 1), :, pl.ds(ch * CL, CL), :]
        pltpu.make_async_copy(gone, gone, send1.at[ch]).wait()
    for half in range(HALVES):
        gone = cb.at[pl.ds(0, (NDEV - 1) * BLK), :]
        pltpu.make_async_copy(gone, gone, send2.at[half]).wait()
    for d in range(2):
        gone = fb.at[pl.ds(0, BINS)]
        pltpu.make_async_copy(gone, gone, sendh.at[d]).wait()
    for copy in outs:
        copy.wait()


def local(raw_echo, chirp_spectrum, azimuth_rate, shift_table, filter_index, tap_table):
    wf, wi, wft, tw_in, tw_out, tw_az = tables()
    chirp = chirp_spectrum.reshape(2, 128, 32).transpose(0, 2, 1) * (1.0 / NRG)
    vmem = pl.BlockSpec(memory_space=pltpu.VMEM)
    smem = pl.BlockSpec(memory_space=pltpu.SMEM)
    hbm = pl.BlockSpec(memory_space=pl.ANY)
    dma = pltpu.SemaphoreType.DMA
    image = pl.pallas_call(
        kernel,
        out_shape=jax.ShapeDtypeStruct((8192, 128), F32),
        in_specs=[hbm, vmem, hbm, vmem, vmem, vmem, vmem, vmem, smem, smem, smem, smem],
        out_specs=hbm,
        scratch_shapes=[
            pltpu.VMEM((NR, 2, LINES, 512), F32),
            pltpu.VMEM((8192, 128), F32),
            pltpu.VMEM((HALVES * HROWS, 128), F32),
            pltpu.VMEM((HALVES * HROWS, 128), F32),
            pltpu.VMEM((3 * BINS, 256, 128), F32),
            pltpu.VMEM((BINS, 2, 128, 128), F32),
            pltpu.VMEM((32, 2, 128, 128), F32),
            pltpu.VMEM((2, 256, 256), F32),
            pltpu.VMEM((128, 128), F32),
            dma,
            dma((CHUNKS,)),
            dma((CHUNKS,)),
            dma((HALVES,)),
            dma((HALVES,)),
            dma((2,)),
            dma((2,)),
            dma((8,)),
        ],
        compiler_params=pltpu.CompilerParams(
            collective_id=0, has_side_effects=True, vmem_limit_bytes=60 * 1024 * 1024
        ),
        cost_estimate=pl.CostEstimate(
            flops=10_000_000_000, bytes_accessed=16 * 1024 * 1024, transcendentals=0
        ),
        name="focus_slab",
    )(
        raw_echo, chirp, tw_out, wf, wi, wft, tw_in, tw_az,
        azimuth_rate, shift_table, filter_index, tap_table,
    )
    image = image.reshape(2, 4, 128, 8, 128).transpose(0, 1, 3, 2, 4)
    return image.reshape(2, BINS, NAZ)


def solution(mesh):
    return jax.shard_map(
        local,
        mesh=mesh,
        in_specs=(
            P(None, "az", "rng"),
            P(),
            P(("rng", "az")),
            P(None, ("rng", "az")),
            P(None, ("rng", "az")),
            P(),
        ),
        out_specs=P(None, ("rng", "az"), None),
        check_vma=False,
    )
```

```python
import functools

import jax
import jax.numpy as jnp
import ml_dtypes
import numpy as np
from jax import lax
from jax.experimental import pallas as pl
from jax.experimental.pallas import tpu as pltpu
from jax.sharding import PartitionSpec as P

NRG = 4096
NAZ = 16384
GROUPS = 16
NFILT = 16
TAPS = 8
HALO = 32

NR = 8
NA = 16
NDEV = NR * NA
BINS = NRG // NDEV
LINES = NAZ // NDEV
CHUNKS = 4
CL = LINES // CHUNKS
HALVES = 2
HL = LINES // HALVES
HB = BINS // HALVES
COL = 8
PLANE = 16
QROWS = 2048

F32 = jnp.float32
BF16 = jnp.bfloat16
MESH = pl.DeviceIdType.MESH


def dft_matrix(sign):
    ids = np.arange(128)
    ang = 2.0 * np.pi * (np.outer(ids, ids) % 128) / 128
    c, s = np.cos(ang), sign * np.sin(ang)
    return np.block([[c, -s], [s, c]])


def split_matrix(m):
    hi = m.astype(ml_dtypes.bfloat16)
    lo = (m - hi.astype(np.float64)).astype(ml_dtypes.bfloat16)
    return np.concatenate([hi, hi, lo], axis=1)


def tables():
    wf = split_matrix(dft_matrix(-1.0))
    wi = split_matrix(dft_matrix(1.0))
    wft = np.ascontiguousarray(wf.T)
    y, xl, xh, zc = np.meshgrid(np.arange(4), np.arange(2), np.arange(2), np.arange(8), indexing="ij")
    order = (64 * xh + 8 * zc + 2 * y + xl).reshape(-1)
    wq = split_matrix(dft_matrix(-1.0)[:, np.concatenate([order, order + 128])])
    k0 = np.arange(32)[:, None]
    b = np.arange(128)[None, :]
    ang = 2.0 * np.pi * (k0 * b % NRG) / NRG
    tw = np.stack([np.cos(ang), -np.sin(ang)])
    tw_in = np.repeat(tw[:, :, None, :], 8, axis=2).astype(np.float32)
    tw_out = np.stack([np.cos(ang), np.sin(ang)], axis=1)
    tw_out = tw_out.reshape(32, 2, 8, 2, 8).transpose(0, 1, 2, 4, 3).reshape(32, 2, 64, 2)
    tw_out = np.repeat(tw_out, HL, axis=3).astype(np.float32)
    ids = np.arange(128)
    ang = 2.0 * np.pi * np.outer(ids, ids) / NAZ
    tw_az = np.stack([np.cos(ang), -np.sin(ang)]).astype(np.float32)
    return wf, wi, wft, wq, tw_in, tw_out, tw_az


def cadd(x, y):
    return (x[0] + y[0], x[1] + y[1])


def csub(x, y):
    return (x[0] - y[0], x[1] - y[1])


def cmul_i(x, sign):
    if sign > 0:
        return (-x[1], x[0])
    return (x[1], -x[0])


def cmul_const(x, num, den, sign):
    num = num % den
    if num == 0:
        return x
    ang = 2.0 * np.pi * num / den
    c, s = float(np.cos(ang)), float(sign * np.sin(ang))
    return (x[0] * c - x[1] * s, x[0] * s + x[1] * c)


def dft4(x, sign):
    a, b = cadd(x[0], x[2]), csub(x[0], x[2])
    c, d = cadd(x[1], x[3]), cmul_i(csub(x[1], x[3]), sign)
    return [cadd(a, c), cadd(b, d), csub(a, c), csub(b, d)]


def dft8(x, sign):
    even = dft4([x[0], x[2], x[4], x[6]], sign)
    odd = dft4([x[1], x[3], x[5], x[7]], sign)
    h = float(np.sqrt(0.5))
    o1 = odd[1]
    o3 = odd[3]
    if sign > 0:
        t1 = ((o1[0] - o1[1]) * h, (o1[0] + o1[1]) * h)
        t3 = ((-o3[0] - o3[1]) * h, (o3[0] - o3[1]) * h)
    else:
        t1 = ((o1[0] + o1[1]) * h, (o1[1] - o1[0]) * h)
        t3 = ((o3[1] - o3[0]) * h, (-o3[0] - o3[1]) * h)
    t = [odd[0], t1, cmul_i(odd[2], sign), t3]
    return [cadd(even[k], t[k]) for k in range(4)] + [csub(even[k], t[k]) for k in range(4)]


def dft32(load, sign):
    cols = []
    for a in range(4):
        y = dft8([load(4 * s + a) for s in range(8)], sign)
        cols.append([cmul_const(y[k], a * k, 32, sign) for k in range(8)])
    out = [None] * 32
    for k in range(8):
        z = dft4([cols[a][k] for a in range(4)], sign)
        for m in range(4):
            out[k + 8 * m] = z[m]
    return out


def three(x, axis):
    hi = x.astype(BF16)
    lo = (x - hi.astype(F32)).astype(BF16)
    return jnp.concatenate([hi, lo, hi], axis=axis)


def dot_nn(a, b):
    return lax.dot_general(a, b, (((1,), (0,)), ((), ())), preferred_element_type=F32)


def dot_nt(a, b):
    return lax.dot_general(a, b, (((1,), (1,)), ((), ())), preferred_element_type=F32)


def swap_halves(x, y):
    low = lax.broadcasted_iota(jnp.int32, x.shape, 1) < 64
    return jnp.where(low, x, pltpu.roll(y, 64, 1)), jnp.where(low, pltpu.roll(x, 64, 1), y)


def dft_pair(w_first, w_ref, x, tw_ref, conj, mixed=False):
    y = dot_nn(w_first[...], three(x, 0))
    if mixed:
        y = jnp.concatenate(swap_halves(y[:, :128], y[:, 128:]), axis=1)
    tr, ti = tw_ref[0], tw_ref[1]
    if conj:
        ti = -ti
    rows = []
    for m in range(2):
        yr = y[:128, 128 * m : 128 * m + 128]
        yi = y[128:, 128 * m : 128 * m + 128]
        rows.append(jnp.concatenate([yr * tr - yi * ti, yr * ti + yi * tr], axis=1))
    return dot_nt(w_ref[...], three(jnp.concatenate(rows, axis=0), 1))


def half_turns(theta):
    m = jnp.floor(theta + 0.5)
    d = theta - m
    half = m * 0.5
    sign = 1.0 - 4.0 * (half - jnp.floor(half))
    x = d * d
    pi = np.pi
    cs = [float((-1) ** n * pi ** (2 * n) / np.prod(np.arange(1.0, 2 * n + 1))) for n in range(7)]
    sn = [
        float((-1) ** n * pi ** (2 * n + 1) / np.prod(np.arange(1.0, 2 * n + 2))) for n in range(6)
    ]
    c = cs[6]
    for n in range(5, -1, -1):
        c = c * x + cs[n]
    s = sn[5]
    for n in range(4, -1, -1):
        s = s * x + sn[n]
    return c * sign, s * d * sign


def kernel(
    raw, chirp, tw_out_hbm, wf, wi, wft, wq, tw_in, tw_az, rate, shift, filt, taps,
    out,
    xb, ub, cb, eb, db, fb, pb, twb, mb, c2b,
    sem_tw, send1, recv1, sendz, recvz, sendy, recvy, sendh, recvh, sem_out,
):
    i = lax.axis_index("rng")
    j = lax.axis_index("az")
    r = i * NA + j
    q = j * NR + i

    zc = lax.rem(j, COL)
    xh = lax.div(j, COL)
    xl = lax.rem(i, 2)
    y = lax.div(i, 2)
    x = 2 * xh + xl
    yx = 4 * y + 2 * xl + xh

    def device(block):
        return (lax.div(block, NA), lax.rem(block, NA))

    def in_column(k):
        return lax.rem(zc + k, COL)

    def in_plane(k):
        to_x = lax.rem(x + k, 4)
        to_y = lax.rem(y + k + lax.div(k, 4), 4)
        to_xl, to_xh = lax.rem(to_x, 2), lax.div(to_x, 2)
        return 4 * to_y + 2 * to_xl + to_xh, (2 * to_y + to_xl, COL * to_xh + zc)

    up = device(lax.rem(r + 1, NDEV))
    down = device(lax.rem(r + NDEV - 1, NDEV))

    barrier = pltpu.get_barrier_semaphore()

    def greet(to):
        pl.semaphore_signal(barrier, inc=1, device_id=to, device_id_type=MESH)

    def greet_column(k, _):
        greet((i, COL * xh + in_column(k)))
        return 0

    def greet_plane(k, _):
        greet(in_plane(k)[1])
        return 0

    lax.fori_loop(1, PLANE, greet_plane, 0)
    lax.fori_loop(1, COL, greet_column, 0)
    greet(up)
    greet(down)
    pl.semaphore_wait(barrier, PLANE - 1 + COL - 1 + 2)

    for ch in range(CHUNKS):

        def lines(block, ch=ch):
            return pl.ds(pl.multiple_of(block * LINES + ch * CL, CL), CL)

        def send_lines(k, _, ch=ch, lines=lines):
            to = lax.rem(i + k, NR)
            pltpu.make_async_remote_copy(
                src_ref=raw.at[:, lines(to), :],
                dst_ref=xb.at[i, :, pl.ds(ch * CL, CL), :],
                send_sem=send1.at[ch],
                recv_sem=recv1.at[ch],
                device_id=(to, j),
                device_id_type=MESH,
            ).start()
            return 0

        lax.fori_loop(1, NR, send_lines, 0)
        pltpu.make_async_copy(
            raw.at[:, lines(i), :], xb.at[i, :, pl.ds(ch * CL, CL), :], recv1.at[ch]
        ).start()

    tw_copy = pltpu.make_async_copy(tw_out_hbm, twb, sem_tw)
    tw_copy.start()

    f1 = lax.broadcasted_iota(jnp.int32, (128, 128), 0)
    f0 = lax.broadcasted_iota(jnp.int32, (128, 128), 1)
    freq = f0 + 128 * f1
    freq = jnp.where(freq >= NAZ // 2, freq - NAZ, freq)
    c = freq.astype(F32) * (1.0 / NAZ)
    c2b[...] = c * c

    def phases(b, _):
        cosine, sine = half_turns(rate[b] * c2b[...])
        pb[b, 0] = cosine * (1.0 / NAZ)
        pb[b, 1] = sine * (1.0 / NAZ)
        return 0

    lax.fori_loop(0, BINS, phases, 0)

    def first_two(ch):
        chunk = xb.at[:, :, pl.ds(ch * CL, CL), :]
        pltpu.make_async_copy(chunk, chunk, recv1.at[ch]).wait()

        def first(t, _, ch=ch):
            rows = pl.ds(pl.multiple_of(ch * CL + t * 8, 8), 8)

            def load(n):
                lanes = pl.ds(128 * (n % 4), 128)
                return (xb[n // 4, 0, rows, lanes], xb[n // 4, 1, rows, lanes])

            res = dft32(load, -1.0)
            for k in range(32):
                lanes = pl.ds(128 * (k % 4), 128)
                tr, ti = tw_in[0, k], tw_in[1, k]
                xr, xi = res[k]
                xb[k // 4, 0, rows, lanes] = xr * tr - xi * ti
                xb[k // 4, 1, rows, lanes] = xr * ti + xi * tr
            return 0

        lax.fori_loop(0, CL // 8, first, 0)

        def second(blk, _, ch=ch):
            rows = pl.ds(ch * CL, CL)
            parts = []
            for m in range(8):
                s = blk * 2 + m // 4
                lanes = pl.ds(128 * (m % 4), 128)
                parts.append(
                    jnp.concatenate([xb[s, 0, rows, lanes], xb[s, 1, rows, lanes]], axis=1)
                )
            y = dot_nn(three(jnp.concatenate(parts, axis=0), 1), wft[...])
            for m in range(8):
                s = blk * 2 + m // 4
                lanes = pl.ds(128 * (m % 4), 128)
                yr = y[m * CL : m * CL + CL, :128]
                yi = y[m * CL : m * CL + CL, 128:]
                hr = chirp[0, pl.ds(blk * 8 + m, 1), :]
                hi = chirp[1, pl.ds(blk * 8 + m, 1), :]
                xb[s, 0, rows, lanes] = yr * hr - yi * hi
                xb[s, 1, rows, lanes] = yr * hi + yi * hr
            return 0

        lax.fori_loop(0, 4, second, 0)

    def third(half):
        lines = pl.ds(half * HL, HL)

        def step(n, _):
            parts = []
            for m in range(4):
                lanes = pl.ds(128 * m, 128)
                parts.append(
                    jnp.concatenate([xb[n, 0, lines, lanes], xb[n, 1, lines, lanes]], axis=1)
                )
            y = dot_nt(wi[...], three(jnp.concatenate(parts, axis=0), 1))
            for h in range(2):
                z = y[:, 128 * h : 128 * h + 128].reshape(16, 2, 8, 128)
                pair = swap_halves(z[:, 0].reshape(128, 128), z[:, 1].reshape(128, 128))
                for m in range(2):
                    k = n * 4 + 2 * h + m
                    zr, zi = pair[m][:64], pair[m][64:]
                    tr, ti = twb[k, 0], twb[k, 1]
                    row = pl.multiple_of(128 * k, 128)
                    ub[pl.ds(row, 64), :] = zr * tr - zi * ti
                    ub[pl.ds(row + 64, 64), :] = zr * ti + zi * tr
            return 0

        lax.fori_loop(0, NR, step, 0)

    def fourth(half, part):
        quarter = 2 * half + part

        def step(n, _):
            own = lax.rem(r, 4)
            beta = (n + own) - 2 * (
                lax.rem(n, 2) * lax.rem(own, 2) + 2 * lax.div(n, 2) * lax.div(own, 2)
            )
            row = pl.multiple_of(8 * (2 * beta + part), 8)

            def load(k):
                return (ub[pl.ds(row + 128 * k, 8), :], ub[pl.ds(row + 128 * k + 64, 8), :])

            res = dft32(load, 1.0)
            for a in range(32):
                base = quarter * QROWS + (4 * (a % 2) + beta) * 256 + (a // 2) * 16
                cb[pl.ds(pl.multiple_of(base, 8), 8), :] = res[a][0]
                cb[pl.ds(pl.multiple_of(base + 8, 8), 8), :] = res[a][1]
            for zh in range(2):
                to = 4 * zh + beta
                rows = pl.ds(pl.multiple_of(quarter * QROWS + to * 256, 256), 256)
                place = eb.at[quarter * COL + zc]

                @pl.when(to != zc)
                def _(rows=rows, to=to, place=place):
                    pltpu.make_async_remote_copy(
                        src_ref=cb.at[rows, :],
                        dst_ref=place,
                        send_sem=sendz.at[quarter],
                        recv_sem=recvz.at[quarter],
                        device_id=(i, COL * xh + to),
                        device_id_type=MESH,
                    ).start()

                @pl.when(to == zc)
                def _(rows=rows, place=place):
                    pltpu.make_async_copy(cb.at[rows, :], place, recvz.at[quarter]).start()

            return 0

        lax.fori_loop(0, 4, step, 0)

    def forward(half, part):
        quarter = 2 * half + part
        landed = eb.at[pl.ds(quarter * COL, COL)]
        pltpu.make_async_copy(landed, landed, recvz.at[quarter]).wait()
        place = db.at[pl.ds(quarter * 128 + yx * COL, COL)]

        def send(k, _):
            to, to_device = in_plane(k)
            pltpu.make_async_remote_copy(
                src_ref=landed.at[:, pl.ds(pl.multiple_of(to * 16, 16), 16), :],
                dst_ref=place,
                send_sem=sendy.at[quarter],
                recv_sem=recvy.at[quarter],
                device_id=to_device,
                device_id_type=MESH,
            ).start()
            return 0

        lax.fori_loop(1, PLANE, send, 0)
        pltpu.make_async_copy(
            landed.at[:, pl.ds(pl.multiple_of(yx * 16, 16), 16), :], place, recvy.at[quarter]
        ).start()

    first_two(0)
    first_two(1)
    tw_copy.wait()
    third(0)
    fourth(0, 0)
    fourth(0, 1)
    first_two(2)
    forward(0, 0)
    first_two(3)
    forward(0, 1)
    third(1)
    fourth(1, 0)
    fourth(1, 1)
    forward(1, 0)
    forward(1, 1)

    def send_halo(row, inner, cross):
        own = fb.at[pl.ds(BINS + row, 2)]
        for place, to, d, edge in ((0, up, 0, COL - 1), (2 * BINS, down, 1, 0)):

            def go(place=place, to=to, d=d):
                pltpu.make_async_remote_copy(
                    src_ref=own,
                    dst_ref=fb.at[pl.ds(place + row, 2)],
                    send_sem=sendh.at[d],
                    recv_sem=recvh.at[d],
                    device_id=to,
                    device_id_type=MESH,
                ).start()

            if inner and cross:
                go()
            elif inner:
                pl.when(zc != edge)(go)
            else:
                pl.when(zc == edge)(go)

    flat = db.reshape(HALVES * HALVES * QROWS, 128)
    for part in range(HALVES):
        for half in range(HALVES):
            landed = db.at[pl.ds((2 * half + part) * 128, 128)]
            pltpu.make_async_copy(landed, landed, recvy.at[2 * half + part]).wait()
        if part == 1:
            for z in range(8):
                send_halo(2 * z, False, True)

        def azimuth(n, part=part):
            cols = []
            for half in range(HALVES):
                base = (2 * half + part) * QROWS + n
                re = flat[pl.ds(base, 128, stride=16), :]
                im = flat[pl.ds(base + 8, 128, stride=16), :]
                cols.append(jnp.concatenate([re, im], axis=0))
            out_pair = dft_pair(wq, wf, jnp.concatenate(cols, axis=1), tw_az, False, mixed=True)
            row = BINS + part * HB + n
            fb[row] = out_pair[:, :128]
            fb[row + 8] = out_pair[:, 128:]

        def azimuth_two(n, _, part=part, azimuth=azimuth):
            azimuth(2 * n)
            azimuth(2 * n + 1)
            send_halo(part * HB + 2 * n, True, part == 1)
            send_halo(part * HB + 2 * n + 8, True, part == 1)
            return 0

        lax.fori_loop(0, HB // 4, azimuth_two, 0)

    for d, place in ((0, 0), (1, 2 * BINS)):
        landed = fb.at[pl.ds(place, BINS)]
        pltpu.make_async_copy(landed, landed, recvh.at[d]).wait()

    @pl.when(r == 0)
    def _():
        def clear(n, _):
            fb[n] = jnp.zeros((256, 128), F32)
            return 0

        lax.fori_loop(0, BINS, clear, 0)

    @pl.when(r == NDEV - 1)
    def _():
        def clear(n, _):
            fb[2 * BINS + n] = jnp.zeros((256, 128), F32)
            return 0

        lax.fori_loop(0, BINS, clear, 0)

    def focus(n, mb):
        for m in range(2):
            b = 2 * n + m
            lanes = pl.ds(128 * m, 128)
            for g in range(GROUPS):
                first_row = BINS + b + shift[g, b] - 4
                which = filt[g, b]
                re, im = pl.ds(8 * g, 8), pl.ds(128 + 8 * g, 8)
                sr = si = None
                for t in range(TAPS):
                    w = taps[t, which]
                    vr = fb[first_row + t, re, :] * w
                    vi = fb[first_row + t, im, :] * w
                    sr = vr if sr is None else sr + vr
                    si = vi if si is None else si + vi
                pc, ps = pb[b, 0, re, :], pb[b, 1, re, :]
                mb[re, lanes] = sr * pc + si * ps
                mb[im, lanes] = si * pc - sr * ps
        y = dft_pair(wi, wi, mb[...], tw_az, True)
        for m in range(2):
            b = 2 * n + m
            for c in range(2):
                base = (c * 4 + lax.div(b, 8)) * 1024 + lax.rem(b, 8)
                ub[pl.ds(base, 128, stride=8), :] = y[128 * c : 128 * c + 128, 128 * m : 128 * m + 128]

    def focus_two(n, _):
        focus(2 * n, mb.at[0])
        focus(2 * n + 1, mb.at[1])
        return 0

    outs = []
    for t in range(4):
        lax.fori_loop(2 * t, 2 * t + 2, focus_two, 0)
        for c in range(2):
            rows = pl.ds((c * 4 + t) * 1024, 1024)
            copy = pltpu.make_async_copy(ub.at[rows, :], out.at[rows, :], sem_out.at[2 * t + c])
            copy.start()
            outs.append(copy)

    for ch in range(CHUNKS):
        gone = xb.at[pl.ds(0, NR - 1), :, pl.ds(ch * CL, CL), :]
        pltpu.make_async_copy(gone, gone, send1.at[ch]).wait()
    for quarter in range(4):
        gone = cb.at[pl.ds(0, (COL - 1) * 256), :]
        pltpu.make_async_copy(gone, gone, sendz.at[quarter]).wait()
        gone = eb.at[pl.ds(0, COL), pl.ds(0, (PLANE - 1) * 16), :]
        pltpu.make_async_copy(gone, gone, sendy.at[quarter]).wait()
    for d in range(2):
        gone = fb.at[pl.ds(0, BINS)]
        pltpu.make_async_copy(gone, gone, sendh.at[d]).wait()
    for copy in outs:
        copy.wait()


def local(raw_echo, chirp_spectrum, azimuth_rate, shift_table, filter_index, tap_table):
    wf, wi, wft, wq, tw_in, tw_out, tw_az = tables()
    chirp = chirp_spectrum.reshape(2, 128, 32).transpose(0, 2, 1) * (1.0 / NRG)
    vmem = pl.BlockSpec(memory_space=pltpu.VMEM)
    smem = pl.BlockSpec(memory_space=pltpu.SMEM)
    hbm = pl.BlockSpec(memory_space=pl.ANY)
    dma = pltpu.SemaphoreType.DMA
    image = pl.pallas_call(
        kernel,
        out_shape=jax.ShapeDtypeStruct((8192, 128), F32),
        in_specs=[hbm, vmem, hbm, vmem, vmem, vmem, vmem, vmem, vmem, smem, smem, smem, smem],
        out_specs=hbm,
        scratch_shapes=[
            pltpu.VMEM((NR, 2, LINES, 512), F32),
            pltpu.VMEM((8192, 128), F32),
            pltpu.VMEM((4 * QROWS, 128), F32),
            pltpu.VMEM((4 * COL, 256, 128), F32),
            pltpu.VMEM((512, 16, 128), F32),
            pltpu.VMEM((3 * BINS, 256, 128), F32),
            pltpu.VMEM((BINS, 2, 128, 128), F32),
            pltpu.VMEM((32, 2, 64, 128), F32),
            pltpu.VMEM((2, 256, 256), F32),
            pltpu.VMEM((128, 128), F32),
            dma,
            dma((CHUNKS,)),
            dma((CHUNKS,)),
            dma((4,)),
            dma((4,)),
            dma((4,)),
            dma((4,)),
            dma((2,)),
            dma((2,)),
            dma((8,)),
        ],
        compiler_params=pltpu.CompilerParams(
            collective_id=0, has_side_effects=True, vmem_limit_bytes=60 * 1024 * 1024
        ),
        cost_estimate=pl.CostEstimate(
            flops=10_000_000_000, bytes_accessed=16 * 1024 * 1024, transcendentals=0
        ),
        name="focus_slab",
    )(
        raw_echo, chirp, tw_out, wf, wi, wft, wq, tw_in, tw_az,
        azimuth_rate, shift_table, filter_index, tap_table.T,
    )
    image = image.reshape(2, 4, 128, 8, 128).transpose(0, 1, 3, 2, 4)
    return image.reshape(2, BINS, NAZ)


def solution(mesh):
    return jax.shard_map(
        local,
        mesh=mesh,
        in_specs=(
            P(None, "az", "rng"),
            P(),
            P(("rng", "az")),
            P(None, ("rng", "az")),
            P(None, ("rng", "az")),
            P(),
        ),
        out_specs=P(None, ("rng", "az"), None),
        check_vma=False,
    )
```

```python
import functools

import jax
import jax.numpy as jnp
import ml_dtypes
import numpy as np
from jax import lax
from jax.experimental import pallas as pl
from jax.experimental.pallas import tpu as pltpu
from jax.sharding import PartitionSpec as P

NRG = 4096
NAZ = 16384
GROUPS = 16
NFILT = 16
TAPS = 8
HALO = 32

NR = 8
NA = 16
NDEV = NR * NA
BINS = NRG // NDEV
LINES = NAZ // NDEV
CHUNKS = 4
CL = LINES // CHUNKS
HALVES = 2
HL = LINES // HALVES
HB = BINS // HALVES
COL = 8
PLANE = 16
QROWS = 2048

F32 = jnp.float32
BF16 = jnp.bfloat16
MESH = pl.DeviceIdType.MESH


def dft_matrix(sign):
    ids = np.arange(128)
    ang = 2.0 * np.pi * (np.outer(ids, ids) % 128) / 128
    c, s = np.cos(ang), sign * np.sin(ang)
    return np.block([[c, -s], [s, c]])


def split_matrix(m):
    hi = m.astype(ml_dtypes.bfloat16)
    lo = (m - hi.astype(np.float64)).astype(ml_dtypes.bfloat16)
    return np.concatenate([hi, hi, lo], axis=1)


def tables():
    wf = split_matrix(dft_matrix(-1.0))
    wi = split_matrix(dft_matrix(1.0))
    lane = np.arange(128)
    k1 = 4 * (lane % 32) + lane // 32
    k1 = np.concatenate([k1, k1 + 128])
    wft = np.ascontiguousarray(split_matrix(dft_matrix(-1.0)[k1]).T)
    b = np.arange(128).reshape(8, 8, 2).transpose(0, 2, 1).reshape(-1)
    wr = split_matrix(dft_matrix(1.0)[np.concatenate([b, b + 128])][:, k1])
    y, xl, xh, zc = np.meshgrid(np.arange(4), np.arange(2), np.arange(2), np.arange(8), indexing="ij")
    order = (64 * xh + 8 * zc + 2 * y + xl).reshape(-1)
    wq = split_matrix(dft_matrix(-1.0)[:, np.concatenate([order, order + 128])])
    k0 = np.arange(32)[:, None]
    b = np.arange(128)[None, :]
    ang = 2.0 * np.pi * (k0 * b % NRG) / NRG
    tw = np.stack([np.cos(ang), -np.sin(ang)])
    tw_in = np.repeat(tw[:, :, None, :], 8, axis=2).astype(np.float32)
    tw_out = np.stack([np.cos(ang), np.sin(ang)], axis=1)
    tw_out = tw_out.reshape(32, 2, 64, 2)
    tw_out = np.repeat(tw_out, HL, axis=3).astype(np.float32)
    ids = np.arange(128)
    ang = 2.0 * np.pi * np.outer(ids, ids) / NAZ
    tw_az = np.stack([np.cos(ang), -np.sin(ang)]).astype(np.float32)
    return wf, wi, wft, wr, wq, tw_in, tw_out, tw_az


def cadd(x, y):
    return (x[0] + y[0], x[1] + y[1])


def csub(x, y):
    return (x[0] - y[0], x[1] - y[1])


def cmul_i(x, sign):
    if sign > 0:
        return (-x[1], x[0])
    return (x[1], -x[0])


def cmul_const(x, num, den, sign):
    num = num % den
    if num == 0:
        return x
    ang = 2.0 * np.pi * num / den
    c, s = float(np.cos(ang)), float(sign * np.sin(ang))
    return (x[0] * c - x[1] * s, x[0] * s + x[1] * c)


def dft4(x, sign):
    a, b = cadd(x[0], x[2]), csub(x[0], x[2])
    c, d = cadd(x[1], x[3]), cmul_i(csub(x[1], x[3]), sign)
    return [cadd(a, c), cadd(b, d), csub(a, c), csub(b, d)]


def dft8(x, sign):
    even = dft4([x[0], x[2], x[4], x[6]], sign)
    odd = dft4([x[1], x[3], x[5], x[7]], sign)
    h = float(np.sqrt(0.5))
    o1 = odd[1]
    o3 = odd[3]
    if sign > 0:
        t1 = ((o1[0] - o1[1]) * h, (o1[0] + o1[1]) * h)
        t3 = ((-o3[0] - o3[1]) * h, (o3[0] - o3[1]) * h)
    else:
        t1 = ((o1[0] + o1[1]) * h, (o1[1] - o1[0]) * h)
        t3 = ((o3[1] - o3[0]) * h, (-o3[0] - o3[1]) * h)
    t = [odd[0], t1, cmul_i(odd[2], sign), t3]
    return [cadd(even[k], t[k]) for k in range(4)] + [csub(even[k], t[k]) for k in range(4)]


def dft32(load, sign):
    cols = []
    for a in range(4):
        y = dft8([load(4 * s + a) for s in range(8)], sign)
        cols.append([cmul_const(y[k], a * k, 32, sign) for k in range(8)])
    out = [None] * 32
    for k in range(8):
        z = dft4([cols[a][k] for a in range(4)], sign)
        for m in range(4):
            out[k + 8 * m] = z[m]
    return out


def three(x, axis):
    hi = x.astype(BF16)
    lo = (x - hi.astype(F32)).astype(BF16)
    return jnp.concatenate([hi, lo, hi], axis=axis)


def dot_nn(a, b):
    return lax.dot_general(a, b, (((1,), (0,)), ((), ())), preferred_element_type=F32)


def dot_nt(a, b):
    return lax.dot_general(a, b, (((1,), (1,)), ((), ())), preferred_element_type=F32)


def swap_halves(x, y):
    low = lax.broadcasted_iota(jnp.int32, x.shape, 1) < 64
    return jnp.where(low, x, pltpu.roll(y, 64, 1)), jnp.where(low, pltpu.roll(x, 64, 1), y)


def dft_pair(w_first, w_ref, x, tw_ref, conj, mixed=False):
    y = dot_nn(w_first[...], three(x, 0))
    if mixed:
        y = jnp.concatenate(swap_halves(y[:, :128], y[:, 128:]), axis=1)
    tr, ti = tw_ref[0], tw_ref[1]
    if conj:
        ti = -ti
    rows = []
    for m in range(2):
        yr = y[:128, 128 * m : 128 * m + 128]
        yi = y[128:, 128 * m : 128 * m + 128]
        rows.append(jnp.concatenate([yr * tr - yi * ti, yr * ti + yi * tr], axis=1))
    return dot_nt(w_ref[...], three(jnp.concatenate(rows, axis=0), 1))


def half_turns(theta):
    m = jnp.floor(theta + 0.5)
    d = theta - m
    half = m * 0.5
    sign = 1.0 - 4.0 * (half - jnp.floor(half))
    x = d * d
    pi = np.pi
    cs = [float((-1) ** n * pi ** (2 * n) / np.prod(np.arange(1.0, 2 * n + 1))) for n in range(7)]
    sn = [
        float((-1) ** n * pi ** (2 * n + 1) / np.prod(np.arange(1.0, 2 * n + 2))) for n in range(6)
    ]
    c = cs[6]
    for n in range(5, -1, -1):
        c = c * x + cs[n]
    s = sn[5]
    for n in range(4, -1, -1):
        s = s * x + sn[n]
    return c * sign, s * d * sign


def kernel(
    raw, spectrum, tw_out_hbm, wf, wi, wft, wr, wq, tw_in, tw_az, rate, shift, filt, taps,
    out,
    xb, ub, cb, eb, db, fb, lb, pb, twb, mb, c2b, chirp,
    sem_tw, send1, recv1, sendz, recvz, sendy, recvy, sendn, recvn, sendf, recvf, sem_out,
):
    i = lax.axis_index("rng")
    j = lax.axis_index("az")
    r = i * NA + j
    q = j * NR + i

    zc = lax.rem(j, COL)
    xh = lax.div(j, COL)
    xl = lax.rem(i, 2)
    y = lax.div(i, 2)
    x = 2 * xh + xl
    core = lax.rem(j, 2)
    yx = 4 * y + 2 * xl + xh

    def device(block):
        return (lax.div(block, NA), lax.rem(block, NA))

    def in_column(k):
        return lax.rem(zc + k, COL)

    def in_plane(k):
        to_x = lax.rem(x + k, 4)
        to_y = lax.rem(y + k + lax.div(k, 4), 4)
        to_xl, to_xh = lax.rem(to_x, 2), lax.div(to_x, 2)
        return 4 * to_y + 2 * to_xl + to_xh, (2 * to_y + to_xl, COL * to_xh + zc)

    near = (i, j + 1 - 2 * core)
    far = device(lax.rem(r + NDEV + 2 * core - 1, NDEV))
    leaves = jnp.logical_or(zc == 0, zc == COL - 1)

    def turned(n, last, flip):
        return n + flip * (last - 2 * n)

    barrier = pltpu.get_barrier_semaphore()

    def greet(to):
        pl.semaphore_signal(barrier, inc=1, device_id=to, device_id_type=MESH)

    def greet_column(k, _):
        greet((i, COL * xh + in_column(k)))
        return 0

    def greet_plane(k, _):
        greet(in_plane(k)[1])
        return 0

    lax.fori_loop(1, PLANE, greet_plane, 0)
    lax.fori_loop(1, COL, greet_column, 0)
    greet(far)
    pl.semaphore_wait(barrier, PLANE - 1 + COL - 1 + 1)

    for ch in range(CHUNKS):

        def lines(block, ch=ch):
            return pl.ds(pl.multiple_of(block * LINES + ch * CL, CL), CL)

        def send_lines(k, _, ch=ch, lines=lines):
            to = lax.rem(i + k, NR)
            pltpu.make_async_remote_copy(
                src_ref=raw.at[:, lines(to), :],
                dst_ref=xb.at[i, :, pl.ds(ch * CL, CL), :],
                send_sem=send1.at[ch],
                recv_sem=recv1.at[ch],
                device_id=(to, j),
                device_id_type=MESH,
            ).start()
            return 0

        lax.fori_loop(1, NR, send_lines, 0)
        pltpu.make_async_copy(
            raw.at[:, lines(i), :], xb.at[i, :, pl.ds(ch * CL, CL), :], recv1.at[ch]
        ).start()

    tw_copy = pltpu.make_async_copy(tw_out_hbm, twb, sem_tw)
    tw_copy.start()

    for part in range(2):
        rows = [spectrum[part : part + 1, 128 * n : 128 * n + 128] for n in range(32)]
        tall = jnp.concatenate(rows + [jnp.zeros((96, 128), F32)], axis=0).T
        spread = tall[:32]
        for n in range(1, 4):
            spread = spread + pltpu.roll(tall[32 * n : 32 * n + 32], 32 * n, 1)
        chirp[part] = spread * (1.0 / NRG)

    f1 = lax.broadcasted_iota(jnp.int32, (128, 128), 0)
    f0 = lax.broadcasted_iota(jnp.int32, (128, 128), 1)
    freq = f0 + 128 * f1
    freq = jnp.where(freq >= NAZ // 2, freq - NAZ, freq)
    c = freq.astype(F32) * (1.0 / NAZ)
    c2b[...] = c * c

    def phases(b, _):
        cosine, sine = half_turns(rate[b] * c2b[...])
        pb[b, 0] = cosine * (1.0 / NAZ)
        pb[b, 1] = sine * (1.0 / NAZ)
        return 0

    lax.fori_loop(0, BINS, phases, 0)

    def first_two(ch):
        chunk = xb.at[:, :, pl.ds(ch * CL, CL), :]
        pltpu.make_async_copy(chunk, chunk, recv1.at[ch]).wait()

        def first(t, _, ch=ch):
            rows = pl.ds(pl.multiple_of(ch * CL + t * 8, 8), 8)

            def load(n):
                lanes = pl.ds(128 * (n % 4), 128)
                return (xb[n // 4, 0, rows, lanes], xb[n // 4, 1, rows, lanes])

            res = dft32(load, -1.0)
            for k in range(32):
                lanes = pl.ds(128 * (k % 4), 128)
                tr, ti = tw_in[0, k], tw_in[1, k]
                xr, xi = res[k]
                xb[k // 4, 0, rows, lanes] = xr * tr - xi * ti
                xb[k // 4, 1, rows, lanes] = xr * ti + xi * tr
            return 0

        lax.fori_loop(0, CL // 8, first, 0)

        def second(blk, _, ch=ch):
            rows = pl.ds(ch * CL, CL)
            parts = []
            for m in range(8):
                s = blk * 2 + m // 4
                lanes = pl.ds(128 * (m % 4), 128)
                parts.append(
                    jnp.concatenate([xb[s, 0, rows, lanes], xb[s, 1, rows, lanes]], axis=1)
                )
            y = dot_nn(three(jnp.concatenate(parts, axis=0), 1), wft[...])
            for m in range(8):
                s = blk * 2 + m // 4
                lanes = pl.ds(128 * (m % 4), 128)
                yr = y[m * CL : m * CL + CL, :128]
                yi = y[m * CL : m * CL + CL, 128:]
                hr = chirp[0, pl.ds(blk * 8 + m, 1), :]
                hi = chirp[1, pl.ds(blk * 8 + m, 1), :]
                xb[s, 0, rows, lanes] = yr * hr - yi * hi
                xb[s, 1, rows, lanes] = yr * hi + yi * hr
            return 0

        lax.fori_loop(0, 4, second, 0)

    def third(half):
        lines = pl.ds(half * HL, HL)

        def step(n, _):
            parts = []
            for m in range(4):
                lanes = pl.ds(128 * m, 128)
                parts.append(
                    jnp.concatenate([xb[n, 0, lines, lanes], xb[n, 1, lines, lanes]], axis=1)
                )
            y = dot_nt(wr[...], three(jnp.concatenate(parts, axis=0), 1))
            for h in range(2):
                z = y[:, 128 * h : 128 * h + 128].reshape(16, 2, 8, 128)
                pair = swap_halves(z[:, 0].reshape(128, 128), z[:, 1].reshape(128, 128))
                for m in range(2):
                    k = n * 4 + 2 * h + m
                    zr, zi = pair[m][:64], pair[m][64:]
                    tr, ti = twb[k, 0], twb[k, 1]
                    row = pl.multiple_of(128 * k, 128)
                    ub[pl.ds(row, 64), :] = zr * tr - zi * ti
                    ub[pl.ds(row + 64, 64), :] = zr * ti + zi * tr
            return 0

        lax.fori_loop(0, NR, step, 0)

    def fourth(half, part):
        quarter = 2 * half + part

        def step(n, _):
            own = lax.rem(r, 4)
            beta = (n + own) - 2 * (
                lax.rem(n, 2) * lax.rem(own, 2) + 2 * lax.div(n, 2) * lax.div(own, 2)
            )
            to_core = lax.rem(beta, 2)
            row = pl.multiple_of(8 * (2 * beta + part + to_core - 2 * part * to_core), 8)

            def load(k):
                return (ub[pl.ds(row + 128 * k, 8), :], ub[pl.ds(row + 128 * k + 64, 8), :])

            res = dft32(load, 1.0)
            for a in range(32):
                base = quarter * QROWS + (4 * (a % 2) + beta) * 256 + (a // 2) * 16
                cb[pl.ds(pl.multiple_of(base, 8), 8), :] = res[a][0]
                cb[pl.ds(pl.multiple_of(base + 8, 8), 8), :] = res[a][1]
            for zh in range(2):
                to = 4 * zh + beta
                rows = pl.ds(pl.multiple_of(quarter * QROWS + to * 256, 256), 256)
                place = eb.at[quarter * COL + zc]

                @pl.when(to != zc)
                def _(rows=rows, to=to, place=place):
                    pltpu.make_async_remote_copy(
                        src_ref=cb.at[rows, :],
                        dst_ref=place,
                        send_sem=sendz.at[quarter],
                        recv_sem=recvz.at[quarter],
                        device_id=(i, COL * xh + to),
                        device_id_type=MESH,
                    ).start()

                @pl.when(to == zc)
                def _(rows=rows, place=place):
                    pltpu.make_async_copy(cb.at[rows, :], place, recvz.at[quarter]).start()

            return 0

        lax.fori_loop(0, 4, step, 0)

    def forward(half, part):
        quarter = 2 * half + part
        landed = eb.at[pl.ds(quarter * COL, COL)]
        pltpu.make_async_copy(landed, landed, recvz.at[quarter]).wait()
        place = db.at[pl.ds(quarter * 128 + yx * COL, COL)]

        def send(k, _):
            to, to_device = in_plane(k)
            pltpu.make_async_remote_copy(
                src_ref=landed.at[:, pl.ds(pl.multiple_of(to * 16, 16), 16), :],
                dst_ref=place,
                send_sem=sendy.at[quarter],
                recv_sem=recvy.at[quarter],
                device_id=to_device,
                device_id_type=MESH,
            ).start()
            return 0

        lax.fori_loop(1, PLANE, send, 0)
        pltpu.make_async_copy(
            landed.at[:, pl.ds(pl.multiple_of(yx * 16, 16), 16), :], place, recvy.at[quarter]
        ).start()

    first_two(0)
    first_two(1)
    tw_copy.wait()
    third(0)
    fourth(0, 0)
    fourth(0, 1)
    first_two(2)
    forward(0, 0)
    first_two(3)
    forward(0, 1)
    third(1)
    fourth(1, 0)
    fourth(1, 1)
    forward(1, 0)
    forward(1, 1)

    def send_near(m):
        row = 2 * turned(m, 15, core)
        pltpu.make_async_remote_copy(
            src_ref=fb.at[pl.ds(BINS + row, 2)],
            dst_ref=fb.at[pl.ds(2 * BINS * core + row, 2)],
            send_sem=sendn,
            recv_sem=recvn,
            device_id=near,
            device_id_type=MESH,
        ).start()

    def send_far(m):
        row = 2 * turned(m, 15, core)
        pltpu.make_async_remote_copy(
            src_ref=fb.at[pl.ds(BINS + row, 2)],
            dst_ref=lb.at[pl.ds(2 * m, 2)],
            send_sem=sendf,
            recv_sem=recvf.at[lax.div(m, 4)],
            device_id=far,
            device_id_type=MESH,
        ).start()

    flat = db.reshape(HALVES * HALVES * QROWS, 128)
    for part in range(HALVES):
        for half in range(HALVES):
            landed = db.at[pl.ds((2 * half + part) * 128, 128)]
            pltpu.make_async_copy(landed, landed, recvy.at[2 * half + part]).wait()

        if part == 1:
            @pl.when(leaves)
            def _():
                def late(m, _):
                    send_far(m)
                    return 0

                lax.fori_loop(0, 8, late, 0)

        def azimuth(m, part=part):
            s = turned(m - 8 * part, 7, core)
            cols = []
            for half in range(HALVES):
                base = (2 * half + part) * QROWS + s
                re = flat[pl.ds(base, 128, stride=16), :]
                im = flat[pl.ds(base + 8, 128, stride=16), :]
                cols.append(jnp.concatenate([re, im], axis=0))
            out_pair = dft_pair(wq, wf, jnp.concatenate(cols, axis=1), tw_az, False, mixed=True)
            row = BINS + 2 * turned(m, 15, core)
            fb[row] = out_pair[:, :128]
            fb[row + 1] = out_pair[:, 128:]

        def azimuth_two(n, _, part=part, azimuth=azimuth):
            m = 8 * part + 2 * n
            azimuth(m)
            azimuth(m + 1)
            for k in range(2):
                send_near(m + k)
                if part == 1:
                    send_far(m + k)
                else:
                    pl.when(jnp.logical_not(leaves))(functools.partial(send_far, m + k))
            return 0

        lax.fori_loop(0, 4, azimuth_two, 0)

    others = fb.at[pl.ds(0, BINS)]
    pltpu.make_async_copy(others, others, recvn).wait()
    outside = jnp.logical_or(r + core == 0, r + core == NDEV)

    def focus(n, mb):
        for m in range(2):
            b = 2 * n + m
            lanes = pl.ds(128 * m, 128)
            for g in range(GROUPS):
                first_row = BINS + b + shift[g, b] - 4
                which = filt[g, b]
                re, im = pl.ds(8 * g, 8), pl.ds(128 + 8 * g, 8)
                sr = si = None
                for t in range(TAPS):
                    w = taps[t, which]
                    vr = fb[first_row + t, re, :] * w
                    vi = fb[first_row + t, im, :] * w
                    sr = vr if sr is None else sr + vr
                    si = vi if si is None else si + vi
                pc, ps = pb[b, 0, re, :], pb[b, 1, re, :]
                mb[re, lanes] = sr * pc + si * ps
                mb[im, lanes] = si * pc - sr * ps
        y = dft_pair(wi, wi, mb[...], tw_az, True)
        for m in range(2):
            b = 2 * n + m
            for c in range(2):
                base = (c * 4 + lax.div(b, 8)) * 1024 + lax.rem(b, 8)
                ub[pl.ds(base, 128, stride=8), :] = y[128 * c : 128 * c + 128, 128 * m : 128 * m + 128]

    for group in range(4):
        rows = lb.at[pl.ds(8 * group, 8)]
        pltpu.make_async_copy(rows, rows, recvf.at[group]).wait()

        def move(n, _, group=group):
            m = 4 * group + n
            row = 2 * turned(m, 15, 1 - core) + 2 * BINS * core
            for k in range(2):
                fb[row + k] = jnp.where(outside, 0.0, lb[2 * m + k])
            return 0

        lax.fori_loop(0, 4, move, 0)

        def focus_two(n, _, group=group):
            for k in range(2):
                focus(turned(4 * group + 2 * n + k, 15, 1 - core), mb.at[k])
            return 0

        lax.fori_loop(0, 2, focus_two, 0)
        eight = turned(group, 3, 1 - core)
        for c in range(2):
            rows = pl.ds(pl.multiple_of((c * 4 + eight) * 1024, 1024), 1024)
            pltpu.make_async_copy(ub.at[rows, :], out.at[rows, :], sem_out.at[2 * group + c]).start()

    for ch in range(CHUNKS):
        gone = xb.at[pl.ds(0, NR - 1), :, pl.ds(ch * CL, CL), :]
        pltpu.make_async_copy(gone, gone, send1.at[ch]).wait()
    for quarter in range(4):
        gone = cb.at[pl.ds(0, (COL - 1) * 256), :]
        pltpu.make_async_copy(gone, gone, sendz.at[quarter]).wait()
        gone = eb.at[pl.ds(0, COL), pl.ds(0, (PLANE - 1) * 16), :]
        pltpu.make_async_copy(gone, gone, sendy.at[quarter]).wait()
    gone = fb.at[pl.ds(BINS, BINS)]
    pltpu.make_async_copy(gone, gone, sendn).wait()
    pltpu.make_async_copy(gone, gone, sendf).wait()
    for n in range(8):
        rows = pl.ds(1024 * n, 1024)
        pltpu.make_async_copy(ub.at[rows, :], out.at[rows, :], sem_out.at[n]).wait()


def local(raw_echo, chirp_spectrum, azimuth_rate, shift_table, filter_index, tap_table):
    wf, wi, wft, wr, wq, tw_in, tw_out, tw_az = tables()
    vmem = pl.BlockSpec(memory_space=pltpu.VMEM)
    smem = pl.BlockSpec(memory_space=pltpu.SMEM)
    hbm = pl.BlockSpec(memory_space=pl.ANY)
    dma = pltpu.SemaphoreType.DMA
    image = pl.pallas_call(
        kernel,
        out_shape=jax.ShapeDtypeStruct((8192, 128), F32),
        in_specs=[hbm, vmem, hbm, vmem, vmem, vmem, vmem, vmem, vmem, vmem, smem, smem, smem, smem],
        out_specs=hbm,
        scratch_shapes=[
            pltpu.VMEM((NR, 2, LINES, 512), F32),
            pltpu.VMEM((8192, 128), F32),
            pltpu.VMEM((4 * QROWS, 128), F32),
            pltpu.VMEM((4 * COL, 256, 128), F32),
            pltpu.VMEM((512, 16, 128), F32),
            pltpu.VMEM((3 * BINS, 256, 128), F32),
            pltpu.VMEM((BINS, 256, 128), F32),
            pltpu.VMEM((BINS, 2, 128, 128), F32),
            pltpu.VMEM((32, 2, 64, 128), F32),
            pltpu.VMEM((2, 256, 256), F32),
            pltpu.VMEM((128, 128), F32),
            pltpu.VMEM((2, 32, 128), F32),
            dma,
            dma((CHUNKS,)),
            dma((CHUNKS,)),
            dma((4,)),
            dma((4,)),
            dma((4,)),
            dma((4,)),
            dma,
            dma,
            dma,
            dma((4,)),
            dma((8,)),
        ],
        compiler_params=pltpu.CompilerParams(
            collective_id=0, has_side_effects=True, vmem_limit_bytes=60 * 1024 * 1024
        ),
        cost_estimate=pl.CostEstimate(
            flops=10_000_000_000, bytes_accessed=16 * 1024 * 1024, transcendentals=0
        ),
        name="focus_slab",
    )(
        raw_echo, chirp_spectrum, tw_out, wf, wi, wft, wr, wq, tw_in, tw_az,
        azimuth_rate, shift_table, filter_index, tap_table.T,
    )
    image = image.reshape(2, 4, 128, 8, 128).transpose(0, 1, 3, 2, 4)
    return image.reshape(2, BINS, NAZ)


def solution(mesh):
    return jax.shard_map(
        local,
        mesh=mesh,
        in_specs=(
            P(None, "az", "rng"),
            P(),
            P(("rng", "az")),
            P(None, ("rng", "az")),
            P(None, ("rng", "az")),
            P(),
        ),
        out_specs=P(None, ("rng", "az"), None),
        check_vma=False,
    )
```

```python
import functools

import jax
import jax.numpy as jnp
import ml_dtypes
import numpy as np
from jax import lax
from jax.experimental import pallas as pl
from jax.experimental.pallas import tpu as pltpu
from jax.sharding import PartitionSpec as P

NRG = 4096
NAZ = 16384
GROUPS = 16
NFILT = 16
TAPS = 8
HALO = 32

NR = 8
NA = 16
NDEV = NR * NA
BINS = NRG // NDEV
LINES = NAZ // NDEV
CHUNKS = 4
CL = LINES // CHUNKS
HALVES = 2
HL = LINES // HALVES
HB = BINS // HALVES
COL = 8
PLANE = 16
QROWS = 2048

F32 = jnp.float32
BF16 = jnp.bfloat16
MESH = pl.DeviceIdType.MESH


def dft_matrix(sign):
    ids = np.arange(128)
    ang = 2.0 * np.pi * (np.outer(ids, ids) % 128) / 128
    c, s = np.cos(ang), sign * np.sin(ang)
    return np.block([[c, -s], [s, c]])


def split_matrix(m):
    hi = m.astype(ml_dtypes.bfloat16)
    lo = (m - hi.astype(np.float64)).astype(ml_dtypes.bfloat16)
    return np.concatenate([hi, hi, lo], axis=1)


def tables():
    wf = split_matrix(dft_matrix(-1.0))
    wi = split_matrix(dft_matrix(1.0))
    lane = np.arange(128)
    k1 = 4 * (lane % 32) + lane // 32
    k1 = np.concatenate([k1, k1 + 128])
    wft = np.ascontiguousarray(split_matrix(dft_matrix(-1.0)[k1]).T)
    b = np.arange(128).reshape(8, 8, 2).transpose(0, 2, 1).reshape(-1)
    wr = split_matrix(dft_matrix(1.0)[np.concatenate([b, b + 128])][:, k1])
    y, xl, xh, zc = np.meshgrid(np.arange(4), np.arange(2), np.arange(2), np.arange(8), indexing="ij")
    order = (64 * xh + 8 * zc + 2 * y + xl).reshape(-1)
    wq = split_matrix(dft_matrix(-1.0)[:, np.concatenate([order, order + 128])])
    k0 = np.arange(32)[:, None]
    b = np.arange(128)[None, :]
    ang = 2.0 * np.pi * (k0 * b % NRG) / NRG
    tw = np.stack([np.cos(ang), -np.sin(ang)])
    tw_in = np.repeat(tw[:, :, None, :], 8, axis=2).astype(np.float32)
    tw_out = np.stack([np.cos(ang), np.sin(ang)], axis=1)
    tw_out = tw_out.reshape(32, 2, 64, 2)
    tw_out = np.repeat(tw_out, HL, axis=3).astype(np.float32)
    ids = np.arange(128)
    ang = 2.0 * np.pi * np.outer(ids, ids) / NAZ
    tw_az = np.stack([np.cos(ang), -np.sin(ang)]).astype(np.float32)
    return wf, wi, wft, wr, wq, tw_in, tw_out, tw_az


def cadd(x, y):
    return (x[0] + y[0], x[1] + y[1])


def csub(x, y):
    return (x[0] - y[0], x[1] - y[1])


def cmul_i(x, sign):
    if sign > 0:
        return (-x[1], x[0])
    return (x[1], -x[0])


def cmul_const(x, num, den, sign):
    num = num % den
    if num == 0:
        return x
    ang = 2.0 * np.pi * num / den
    c, s = float(np.cos(ang)), float(sign * np.sin(ang))
    return (x[0] * c - x[1] * s, x[0] * s + x[1] * c)


def dft4(x, sign):
    a, b = cadd(x[0], x[2]), csub(x[0], x[2])
    c, d = cadd(x[1], x[3]), cmul_i(csub(x[1], x[3]), sign)
    return [cadd(a, c), cadd(b, d), csub(a, c), csub(b, d)]


def dft8(x, sign):
    even = dft4([x[0], x[2], x[4], x[6]], sign)
    odd = dft4([x[1], x[3], x[5], x[7]], sign)
    h = float(np.sqrt(0.5))
    o1 = odd[1]
    o3 = odd[3]
    if sign > 0:
        t1 = ((o1[0] - o1[1]) * h, (o1[0] + o1[1]) * h)
        t3 = ((-o3[0] - o3[1]) * h, (o3[0] - o3[1]) * h)
    else:
        t1 = ((o1[0] + o1[1]) * h, (o1[1] - o1[0]) * h)
        t3 = ((o3[1] - o3[0]) * h, (-o3[0] - o3[1]) * h)
    t = [odd[0], t1, cmul_i(odd[2], sign), t3]
    return [cadd(even[k], t[k]) for k in range(4)] + [csub(even[k], t[k]) for k in range(4)]


def dft32(load, sign):
    cols = []
    for a in range(4):
        y = dft8([load(4 * s + a) for s in range(8)], sign)
        cols.append([cmul_const(y[k], a * k, 32, sign) for k in range(8)])
    out = [None] * 32
    for k in range(8):
        z = dft4([cols[a][k] for a in range(4)], sign)
        for m in range(4):
            out[k + 8 * m] = z[m]
    return out


def three(x, axis):
    hi = x.astype(BF16)
    lo = (x - hi.astype(F32)).astype(BF16)
    return jnp.concatenate([hi, lo, hi], axis=axis)


def dot_nn(a, b):
    return lax.dot_general(a, b, (((1,), (0,)), ((), ())), preferred_element_type=F32)


def dot_nt(a, b):
    return lax.dot_general(a, b, (((1,), (1,)), ((), ())), preferred_element_type=F32)


def swap_halves(x, y):
    low = lax.broadcasted_iota(jnp.int32, x.shape, 1) < 64
    return jnp.where(low, x, pltpu.roll(y, 64, 1)), jnp.where(low, pltpu.roll(x, 64, 1), y)


def dft_pair(w_first, w_ref, x, tw_ref, conj, mixed=False):
    y = dot_nn(w_first[...], three(x, 0))
    if mixed:
        y = jnp.concatenate(swap_halves(y[:, :128], y[:, 128:]), axis=1)
    tr, ti = tw_ref[0], tw_ref[1]
    if conj:
        ti = -ti
    rows = []
    for m in range(2):
        yr = y[:128, 128 * m : 128 * m + 128]
        yi = y[128:, 128 * m : 128 * m + 128]
        rows.append(jnp.concatenate([yr * tr - yi * ti, yr * ti + yi * tr], axis=1))
    return dot_nt(w_ref[...], three(jnp.concatenate(rows, axis=0), 1))


def half_turns(theta):
    m = jnp.floor(theta + 0.5)
    d = theta - m
    half = m * 0.5
    sign = 1.0 - 4.0 * (half - jnp.floor(half))
    x = d * d
    pi = np.pi
    cs = [float((-1) ** n * pi ** (2 * n) / np.prod(np.arange(1.0, 2 * n + 1))) for n in range(7)]
    sn = [
        float((-1) ** n * pi ** (2 * n + 1) / np.prod(np.arange(1.0, 2 * n + 2))) for n in range(6)
    ]
    c = cs[6]
    for n in range(5, -1, -1):
        c = c * x + cs[n]
    s = sn[5]
    for n in range(4, -1, -1):
        s = s * x + sn[n]
    return c * sign, s * d * sign


def kernel(
    raw, spectrum_hbm, tw_out_hbm, wf_hbm, wi_hbm, wft_hbm, wr_hbm, wq_hbm, tw_in_hbm, tw_az_hbm, rate, shift, filt, taps,
    out,
    xb, ub, cb, eb, db, fb, lb, pb, twb, mb, c2b, chirp,
    spectrum, wf, wi, wft, wr, wq, tw_in, tw_az, sem_in,
    sem_tw, send1, recv1, sendz, recvz, sendy, recvy, sendn, recvn, sendf, recvf, sem_out,
):
    i = lax.axis_index("rng")
    j = lax.axis_index("az")
    r = i * NA + j
    q = j * NR + i

    zc = lax.rem(j, COL)
    xh = lax.div(j, COL)
    xl = lax.rem(i, 2)
    y = lax.div(i, 2)
    x = 2 * xh + xl
    core = lax.rem(j, 2)
    yx = 4 * y + 2 * xl + xh

    def device(block):
        return (lax.div(block, NA), lax.rem(block, NA))

    def in_column(k):
        return lax.rem(zc + k, COL)

    def in_plane(k):
        to_x = lax.rem(x + k, 4)
        to_y = lax.rem(y + k + lax.div(k, 4), 4)
        to_xl, to_xh = lax.rem(to_x, 2), lax.div(to_x, 2)
        return 4 * to_y + 2 * to_xl + to_xh, (2 * to_y + to_xl, COL * to_xh + zc)

    near = (i, j + 1 - 2 * core)
    far = device(lax.rem(r + NDEV + 2 * core - 1, NDEV))
    leaves = jnp.logical_or(zc == 0, zc == COL - 1)

    def turned(n, last, flip):
        return n + flip * (last - 2 * n)

    barrier = pltpu.get_barrier_semaphore()

    def greet(to):
        pl.semaphore_signal(barrier, inc=1, device_id=to, device_id_type=MESH)

    def greet_column(k, _):
        greet((i, COL * xh + in_column(k)))
        return 0

    def greet_plane(k, _):
        greet(in_plane(k)[1])
        return 0

    lax.fori_loop(1, PLANE, greet_plane, 0)
    lax.fori_loop(1, COL, greet_column, 0)
    greet(far)
    pl.semaphore_wait(barrier, PLANE - 1 + COL - 1 + 1)

    for ch in range(CHUNKS):

        def lines(block, ch=ch):
            return pl.ds(pl.multiple_of(block * LINES + ch * CL, CL), CL)

        def send_lines(k, _, ch=ch, lines=lines):
            to = lax.rem(i + k, NR)
            pltpu.make_async_remote_copy(
                src_ref=raw.at[:, lines(to), :],
                dst_ref=xb.at[i, :, pl.ds(ch * CL, CL), :],
                send_sem=send1.at[ch],
                recv_sem=recv1.at[ch],
                device_id=(to, j),
                device_id_type=MESH,
            ).start()
            return 0

        lax.fori_loop(1, NR, send_lines, 0)
        pltpu.make_async_copy(
            raw.at[:, lines(i), :], xb.at[i, :, pl.ds(ch * CL, CL), :], recv1.at[ch]
        ).start()

    tw_copy = pltpu.make_async_copy(tw_out_hbm, twb, sem_tw)
    tw_copy.start()
    loads = [
        pltpu.make_async_copy(source, place, sem_in.at[n])
        for n, (source, place) in enumerate(
            (
                (spectrum_hbm, spectrum), (wft_hbm, wft), (tw_in_hbm, tw_in), (wr_hbm, wr),
                (wq_hbm, wq), (wf_hbm, wf), (tw_az_hbm, tw_az), (wi_hbm, wi),
            )
        )
    ]
    for load in loads:
        load.start()
    loads[0].wait()

    for part in range(2):
        rows = [spectrum[part : part + 1, 128 * n : 128 * n + 128] for n in range(32)]
        tall = jnp.concatenate(rows + [jnp.zeros((96, 128), F32)], axis=0).T
        spread = tall[:32]
        for n in range(1, 4):
            spread = spread + pltpu.roll(tall[32 * n : 32 * n + 32], 32 * n, 1)
        chirp[part] = spread * (1.0 / NRG)

    f1 = lax.broadcasted_iota(jnp.int32, (128, 128), 0)
    f0 = lax.broadcasted_iota(jnp.int32, (128, 128), 1)
    freq = f0 + 128 * f1
    freq = jnp.where(freq >= NAZ // 2, freq - NAZ, freq)
    c = freq.astype(F32) * (1.0 / NAZ)
    c2b[...] = c * c

    def phases(b, _):
        cosine, sine = half_turns(rate[b] * c2b[...])
        pb[b, 0] = cosine * (1.0 / NAZ)
        pb[b, 1] = sine * (1.0 / NAZ)
        return 0

    lax.fori_loop(0, BINS, phases, 0)

    def first_two(ch):
        chunk = xb.at[:, :, pl.ds(ch * CL, CL), :]
        pltpu.make_async_copy(chunk, chunk, recv1.at[ch]).wait()

        def first(t, _, ch=ch):
            rows = pl.ds(pl.multiple_of(ch * CL + t * 8, 8), 8)

            def load(n):
                lanes = pl.ds(128 * (n % 4), 128)
                return (xb[n // 4, 0, rows, lanes], xb[n // 4, 1, rows, lanes])

            res = dft32(load, -1.0)
            for k in range(32):
                lanes = pl.ds(128 * (k % 4), 128)
                tr, ti = tw_in[0, k], tw_in[1, k]
                xr, xi = res[k]
                xb[k // 4, 0, rows, lanes] = xr * tr - xi * ti
                xb[k // 4, 1, rows, lanes] = xr * ti + xi * tr
            return 0

        lax.fori_loop(0, CL // 8, first, 0)

        def second(blk, _, ch=ch):
            rows = pl.ds(ch * CL, CL)
            parts = []
            for m in range(8):
                s = blk * 2 + m // 4
                lanes = pl.ds(128 * (m % 4), 128)
                parts.append(
                    jnp.concatenate([xb[s, 0, rows, lanes], xb[s, 1, rows, lanes]], axis=1)
                )
            y = dot_nn(three(jnp.concatenate(parts, axis=0), 1), wft[...])
            for m in range(8):
                s = blk * 2 + m // 4
                lanes = pl.ds(128 * (m % 4), 128)
                yr = y[m * CL : m * CL + CL, :128]
                yi = y[m * CL : m * CL + CL, 128:]
                hr = chirp[0, pl.ds(blk * 8 + m, 1), :]
                hi = chirp[1, pl.ds(blk * 8 + m, 1), :]
                xb[s, 0, rows, lanes] = yr * hr - yi * hi
                xb[s, 1, rows, lanes] = yr * hi + yi * hr
            return 0

        lax.fori_loop(0, 4, second, 0)

    def third(half):
        lines = pl.ds(half * HL, HL)

        def step(n, _):
            parts = []
            for m in range(4):
                lanes = pl.ds(128 * m, 128)
                parts.append(
                    jnp.concatenate([xb[n, 0, lines, lanes], xb[n, 1, lines, lanes]], axis=1)
                )
            y = dot_nt(wr[...], three(jnp.concatenate(parts, axis=0), 1))
            for h in range(2):
                z = y[:, 128 * h : 128 * h + 128].reshape(16, 2, 8, 128)
                pair = swap_halves(z[:, 0].reshape(128, 128), z[:, 1].reshape(128, 128))
                for m in range(2):
                    k = n * 4 + 2 * h + m
                    zr, zi = pair[m][:64], pair[m][64:]
                    tr, ti = twb[k, 0], twb[k, 1]
                    row = pl.multiple_of(128 * k, 128)
                    ub[pl.ds(row, 64), :] = zr * tr - zi * ti
                    ub[pl.ds(row + 64, 64), :] = zr * ti + zi * tr
            return 0

        lax.fori_loop(0, NR, step, 0)

    def fourth(half, part):
        quarter = 2 * half + part

        def step(n, _):
            own = lax.rem(r, 4)
            beta = (n + own) - 2 * (
                lax.rem(n, 2) * lax.rem(own, 2) + 2 * lax.div(n, 2) * lax.div(own, 2)
            )
            to_core = lax.rem(beta, 2)
            row = pl.multiple_of(8 * (2 * beta + part + to_core - 2 * part * to_core), 8)

            def load(k):
                return (ub[pl.ds(row + 128 * k, 8), :], ub[pl.ds(row + 128 * k + 64, 8), :])

            res = dft32(load, 1.0)
            for a in range(32):
                base = quarter * QROWS + (4 * (a % 2) + beta) * 256 + (a // 2) * 16
                cb[pl.ds(pl.multiple_of(base, 8), 8), :] = res[a][0]
                cb[pl.ds(pl.multiple_of(base + 8, 8), 8), :] = res[a][1]
            for zh in range(2):
                to = 4 * zh + beta
                rows = pl.ds(pl.multiple_of(quarter * QROWS + to * 256, 256), 256)
                place = eb.at[quarter * COL + zc]

                @pl.when(to != zc)
                def _(rows=rows, to=to, place=place):
                    pltpu.make_async_remote_copy(
                        src_ref=cb.at[rows, :],
                        dst_ref=place,
                        send_sem=sendz.at[quarter],
                        recv_sem=recvz.at[quarter],
                        device_id=(i, COL * xh + to),
                        device_id_type=MESH,
                    ).start()

                @pl.when(to == zc)
                def _(rows=rows, place=place):
                    pltpu.make_async_copy(cb.at[rows, :], place, recvz.at[quarter]).start()

            return 0

        lax.fori_loop(0, 4, step, 0)

    def forward(half, part):
        quarter = 2 * half + part
        landed = eb.at[pl.ds(quarter * COL, COL)]
        pltpu.make_async_copy(landed, landed, recvz.at[quarter]).wait()
        place = db.at[pl.ds(quarter * 128 + yx * COL, COL)]

        def send(k, _):
            to, to_device = in_plane(k)
            pltpu.make_async_remote_copy(
                src_ref=landed.at[:, pl.ds(pl.multiple_of(to * 16, 16), 16), :],
                dst_ref=place,
                send_sem=sendy.at[quarter],
                recv_sem=recvy.at[quarter],
                device_id=to_device,
                device_id_type=MESH,
            ).start()
            return 0

        lax.fori_loop(1, PLANE, send, 0)
        pltpu.make_async_copy(
            landed.at[:, pl.ds(pl.multiple_of(yx * 16, 16), 16), :], place, recvy.at[quarter]
        ).start()

    for load in loads[1:]:
        load.wait()
    first_two(0)
    first_two(1)
    tw_copy.wait()
    third(0)
    fourth(0, 0)
    fourth(0, 1)
    first_two(2)
    forward(0, 0)
    first_two(3)
    forward(0, 1)
    third(1)
    fourth(1, 0)
    fourth(1, 1)
    forward(1, 0)
    forward(1, 1)

    def send_near(m):
        row = 2 * turned(m, 15, core)
        pltpu.make_async_remote_copy(
            src_ref=fb.at[pl.ds(BINS + row, 2)],
            dst_ref=fb.at[pl.ds(2 * BINS * core + row, 2)],
            send_sem=sendn,
            recv_sem=recvn,
            device_id=near,
            device_id_type=MESH,
        ).start()

    def send_far(m):
        row = 2 * turned(m, 15, core)
        pltpu.make_async_remote_copy(
            src_ref=fb.at[pl.ds(BINS + row, 2)],
            dst_ref=lb.at[pl.ds(2 * m, 2)],
            send_sem=sendf,
            recv_sem=recvf.at[lax.div(m, 2)],
            device_id=far,
            device_id_type=MESH,
        ).start()

    flat = db.reshape(HALVES * HALVES * QROWS, 128)
    for part in range(HALVES):
        for half in range(HALVES):
            landed = db.at[pl.ds((2 * half + part) * 128, 128)]
            pltpu.make_async_copy(landed, landed, recvy.at[2 * half + part]).wait()

        if part == 1:
            @pl.when(leaves)
            def _():
                def late(m, _):
                    send_far(m)
                    return 0

                lax.fori_loop(0, 8, late, 0)

        def azimuth(m, part=part):
            s = turned(m - 8 * part, 7, core)
            cols = []
            for half in range(HALVES):
                base = (2 * half + part) * QROWS + s
                re = flat[pl.ds(base, 128, stride=16), :]
                im = flat[pl.ds(base + 8, 128, stride=16), :]
                cols.append(jnp.concatenate([re, im], axis=0))
            out_pair = dft_pair(wq, wf, jnp.concatenate(cols, axis=1), tw_az, False, mixed=True)
            row = BINS + 2 * turned(m, 15, core)
            fb[row] = out_pair[:, :128]
            fb[row + 1] = out_pair[:, 128:]

        def azimuth_two(n, _, part=part, azimuth=azimuth):
            m = 8 * part + 2 * n
            azimuth(m)
            azimuth(m + 1)
            for k in range(2):
                send_near(m + k)
                if part == 1:
                    send_far(m + k)
                else:
                    pl.when(jnp.logical_not(leaves))(functools.partial(send_far, m + k))
            return 0

        lax.fori_loop(0, 4, azimuth_two, 0)

    others = fb.at[pl.ds(0, BINS)]
    pltpu.make_async_copy(others, others, recvn).wait()
    outside = jnp.logical_or(r + core == 0, r + core == NDEV)

    def focus(n, mb):
        for m in range(2):
            b = 2 * n + m
            lanes = pl.ds(128 * m, 128)
            for g in range(GROUPS):
                first_row = BINS + b + shift[g, b] - 4
                which = filt[g, b]
                re, im = pl.ds(8 * g, 8), pl.ds(128 + 8 * g, 8)
                sr = si = None
                for t in range(TAPS):
                    w = taps[t, which]
                    vr = fb[first_row + t, re, :] * w
                    vi = fb[first_row + t, im, :] * w
                    sr = vr if sr is None else sr + vr
                    si = vi if si is None else si + vi
                pc, ps = pb[b, 0, re, :], pb[b, 1, re, :]
                mb[re, lanes] = sr * pc + si * ps
                mb[im, lanes] = si * pc - sr * ps
        y = dft_pair(wi, wi, mb[...], tw_az, True)
        for m in range(2):
            b = 2 * n + m
            for c in range(2):
                base = (c * 4 + lax.div(b, 8)) * 1024 + lax.rem(b, 8)
                ub[pl.ds(base, 128, stride=8), :] = y[128 * c : 128 * c + 128, 128 * m : 128 * m + 128]

    for group in range(8):
        rows = lb.at[pl.ds(4 * group, 4)]
        pltpu.make_async_copy(rows, rows, recvf.at[group]).wait()
        for k in range(2):
            m = 2 * group + k
            row = 2 * turned(m, 15, 1 - core) + 2 * BINS * core
            for h in range(2):
                fb[row + h] = jnp.where(outside, 0.0, lb[2 * m + h])
        for k in range(2):
            focus(turned(2 * group + k, 15, 1 - core), mb.at[k])
        if group % 2 == 1:
            eight = turned(group // 2, 3, 1 - core)
            for c in range(2):
                rows = pl.ds(pl.multiple_of((c * 4 + eight) * 1024, 1024), 1024)
                sem = sem_out.at[group - 1 + c]
                pltpu.make_async_copy(ub.at[rows, :], out.at[rows, :], sem).start()

    for ch in range(CHUNKS):
        gone = xb.at[pl.ds(0, NR - 1), :, pl.ds(ch * CL, CL), :]
        pltpu.make_async_copy(gone, gone, send1.at[ch]).wait()
    for quarter in range(4):
        gone = cb.at[pl.ds(0, (COL - 1) * 256), :]
        pltpu.make_async_copy(gone, gone, sendz.at[quarter]).wait()
        gone = eb.at[pl.ds(0, COL), pl.ds(0, (PLANE - 1) * 16), :]
        pltpu.make_async_copy(gone, gone, sendy.at[quarter]).wait()
    gone = fb.at[pl.ds(BINS, BINS)]
    pltpu.make_async_copy(gone, gone, sendn).wait()
    pltpu.make_async_copy(gone, gone, sendf).wait()
    for n in range(8):
        rows = pl.ds(1024 * n, 1024)
        pltpu.make_async_copy(ub.at[rows, :], out.at[rows, :], sem_out.at[n]).wait()


def local(raw_echo, chirp_spectrum, azimuth_rate, shift_table, filter_index, tap_table):
    wf, wi, wft, wr, wq, tw_in, tw_out, tw_az = tables()
    smem = pl.BlockSpec(memory_space=pltpu.SMEM)
    hbm = pl.BlockSpec(memory_space=pl.ANY)
    dma = pltpu.SemaphoreType.DMA
    image = pl.pallas_call(
        kernel,
        out_shape=jax.ShapeDtypeStruct((8192, 128), F32),
        in_specs=[hbm] * 10 + [smem] * 4,
        out_specs=hbm,
        scratch_shapes=[
            pltpu.VMEM((NR, 2, LINES, 512), F32),
            pltpu.VMEM((8192, 128), F32),
            pltpu.VMEM((4 * QROWS, 128), F32),
            pltpu.VMEM((4 * COL, 256, 128), F32),
            pltpu.VMEM((512, 16, 128), F32),
            pltpu.VMEM((3 * BINS, 256, 128), F32),
            pltpu.VMEM((BINS, 256, 128), F32),
            pltpu.VMEM((BINS, 2, 128, 128), F32),
            pltpu.VMEM((32, 2, 64, 128), F32),
            pltpu.VMEM((2, 256, 256), F32),
            pltpu.VMEM((128, 128), F32),
            pltpu.VMEM((2, 32, 128), F32),
            pltpu.VMEM((2, NRG), F32),
            pltpu.VMEM((256, 768), BF16),
            pltpu.VMEM((256, 768), BF16),
            pltpu.VMEM((768, 256), BF16),
            pltpu.VMEM((256, 768), BF16),
            pltpu.VMEM((256, 768), BF16),
            pltpu.VMEM((2, 32, 8, 128), F32),
            pltpu.VMEM((2, 128, 128), F32),
            dma((8,)),
            dma,
            dma((CHUNKS,)),
            dma((CHUNKS,)),
            dma((4,)),
            dma((4,)),
            dma((4,)),
            dma((4,)),
            dma,
            dma,
            dma,
            dma((8,)),
            dma((8,)),
        ],
        compiler_params=pltpu.CompilerParams(
            collective_id=0, has_side_effects=True, vmem_limit_bytes=60 * 1024 * 1024
        ),
        cost_estimate=pl.CostEstimate(
            flops=10_000_000_000, bytes_accessed=16 * 1024 * 1024, transcendentals=0
        ),
        name="focus_slab",
    )(
        raw_echo, chirp_spectrum, tw_out, wf, wi, wft, wr, wq, tw_in, tw_az,
        azimuth_rate, shift_table, filter_index, tap_table.T,
    )
    image = image.reshape(2, 4, 128, 8, 128).transpose(0, 1, 3, 2, 4)
    return image.reshape(2, BINS, NAZ)


def solution(mesh):
    return jax.shard_map(
        local,
        mesh=mesh,
        in_specs=(
            P(None, "az", "rng"),
            P(),
            P(("rng", "az")),
            P(None, ("rng", "az")),
            P(None, ("rng", "az")),
            P(),
        ),
        out_specs=P(None, ("rng", "az"), None),
        check_vma=False,
    )
```

```python
import functools

import jax
import jax.numpy as jnp
import ml_dtypes
import numpy as np
from jax import lax
from jax.experimental import pallas as pl
from jax.experimental.pallas import tpu as pltpu
from jax.sharding import PartitionSpec as P

NRG = 4096
NAZ = 16384
GROUPS = 16
NFILT = 16
TAPS = 8
HALO = 32

NR = 8
NA = 16
NDEV = NR * NA
BINS = NRG // NDEV
LINES = NAZ // NDEV
CHUNKS = 4
CL = LINES // CHUNKS
HALVES = 2
HL = LINES // HALVES
HB = BINS // HALVES
COL = 8
PLANE = 16
QROWS = 2048

F32 = jnp.float32
BF16 = jnp.bfloat16
MESH = pl.DeviceIdType.MESH


def dft_matrix(sign):
    ids = np.arange(128)
    ang = 2.0 * np.pi * (np.outer(ids, ids) % 128) / 128
    c, s = np.cos(ang), sign * np.sin(ang)
    return np.block([[c, -s], [s, c]])


def split_matrix(m):
    hi = m.astype(ml_dtypes.bfloat16)
    lo = (m - hi.astype(np.float64)).astype(ml_dtypes.bfloat16)
    return np.concatenate([hi, hi, lo], axis=1)


def tables():
    wf = split_matrix(dft_matrix(-1.0))
    wi = split_matrix(dft_matrix(1.0))
    lane = np.arange(128)
    k1 = 4 * (lane % 32) + lane // 32
    k1 = np.concatenate([k1, k1 + 128])
    wft = np.ascontiguousarray(split_matrix(dft_matrix(-1.0)[k1]).T)
    b = np.arange(128).reshape(8, 8, 2).transpose(0, 2, 1).reshape(-1)
    wr = split_matrix(dft_matrix(1.0)[np.concatenate([b, b + 128])][:, k1])
    y, xl, xh, zc = np.meshgrid(np.arange(4), np.arange(2), np.arange(2), np.arange(8), indexing="ij")
    order = (64 * xh + 8 * zc + 2 * y + xl).reshape(-1)
    wq = split_matrix(dft_matrix(-1.0)[:, np.concatenate([order, order + 128])])
    k0 = np.arange(32)[:, None]
    b = np.arange(128)[None, :]
    ang = 2.0 * np.pi * (k0 * b % NRG) / NRG
    tw = np.stack([np.cos(ang), -np.sin(ang)])
    tw_in = np.repeat(tw[:, :, None, :], 8, axis=2).astype(np.float32)
    tw_out = np.stack([np.cos(ang), np.sin(ang)], axis=1)
    tw_out = tw_out.reshape(32, 2, 64, 2)
    tw_out = np.repeat(tw_out, HL, axis=3).astype(np.float32)
    ids = np.arange(128)
    ang = 2.0 * np.pi * np.outer(ids, ids) / NAZ
    tw_az = np.stack([np.cos(ang), -np.sin(ang)]).astype(np.float32)
    return wf, wi, wft, wr, wq, tw_in, tw_out, tw_az


def cadd(x, y):
    return (x[0] + y[0], x[1] + y[1])


def csub(x, y):
    return (x[0] - y[0], x[1] - y[1])


def cmul_i(x, sign):
    if sign > 0:
        return (-x[1], x[0])
    return (x[1], -x[0])


def cmul_const(x, num, den, sign):
    num = num % den
    if num == 0:
        return x
    ang = 2.0 * np.pi * num / den
    c, s = float(np.cos(ang)), float(sign * np.sin(ang))
    return (x[0] * c - x[1] * s, x[0] * s + x[1] * c)


def dft4(x, sign):
    a, b = cadd(x[0], x[2]), csub(x[0], x[2])
    c, d = cadd(x[1], x[3]), cmul_i(csub(x[1], x[3]), sign)
    return [cadd(a, c), cadd(b, d), csub(a, c), csub(b, d)]


def dft8(x, sign):
    even = dft4([x[0], x[2], x[4], x[6]], sign)
    odd = dft4([x[1], x[3], x[5], x[7]], sign)
    h = float(np.sqrt(0.5))
    o1 = odd[1]
    o3 = odd[3]
    if sign > 0:
        t1 = ((o1[0] - o1[1]) * h, (o1[0] + o1[1]) * h)
        t3 = ((-o3[0] - o3[1]) * h, (o3[0] - o3[1]) * h)
    else:
        t1 = ((o1[0] + o1[1]) * h, (o1[1] - o1[0]) * h)
        t3 = ((o3[1] - o3[0]) * h, (-o3[0] - o3[1]) * h)
    t = [odd[0], t1, cmul_i(odd[2], sign), t3]
    return [cadd(even[k], t[k]) for k in range(4)] + [csub(even[k], t[k]) for k in range(4)]


def dft32(load, sign):
    cols = []
    for a in range(4):
        y = dft8([load(4 * s + a) for s in range(8)], sign)
        cols.append([cmul_const(y[k], a * k, 32, sign) for k in range(8)])
    out = [None] * 32
    for k in range(8):
        z = dft4([cols[a][k] for a in range(4)], sign)
        for m in range(4):
            out[k + 8 * m] = z[m]
    return out


def three(x, axis):
    hi = x.astype(BF16)
    lo = (x - hi.astype(F32)).astype(BF16)
    return jnp.concatenate([hi, lo, hi], axis=axis)


def dot_nn(a, b):
    return lax.dot_general(a, b, (((1,), (0,)), ((), ())), preferred_element_type=F32)


def dot_nt(a, b):
    return lax.dot_general(a, b, (((1,), (1,)), ((), ())), preferred_element_type=F32)


def swap_halves(x, y):
    low = lax.broadcasted_iota(jnp.int32, x.shape, 1) < 64
    return jnp.where(low, x, pltpu.roll(y, 64, 1)), jnp.where(low, pltpu.roll(x, 64, 1), y)


def dft_pair(w_first, w_ref, x, tw_ref, conj, mixed=False):
    y = dot_nn(w_first[...], three(x, 0))
    if mixed:
        y = jnp.concatenate(swap_halves(y[:, :128], y[:, 128:]), axis=1)
    tr, ti = tw_ref[0], tw_ref[1]
    if conj:
        ti = -ti
    rows = []
    for m in range(2):
        yr = y[:128, 128 * m : 128 * m + 128]
        yi = y[128:, 128 * m : 128 * m + 128]
        rows.append(jnp.concatenate([yr * tr - yi * ti, yr * ti + yi * tr], axis=1))
    return dot_nt(w_ref[...], three(jnp.concatenate(rows, axis=0), 1))


def half_turns(theta):
    m = jnp.floor(theta + 0.5)
    d = theta - m
    half = m * 0.5
    sign = 1.0 - 4.0 * (half - jnp.floor(half))
    x = d * d
    pi = np.pi
    cs = [float((-1) ** n * pi ** (2 * n) / np.prod(np.arange(1.0, 2 * n + 1))) for n in range(7)]
    sn = [
        float((-1) ** n * pi ** (2 * n + 1) / np.prod(np.arange(1.0, 2 * n + 2))) for n in range(6)
    ]
    c = cs[6]
    for n in range(5, -1, -1):
        c = c * x + cs[n]
    s = sn[5]
    for n in range(4, -1, -1):
        s = s * x + sn[n]
    return c * sign, s * d * sign


def kernel(
    raw, spectrum_hbm, tw_out_hbm, wf_hbm, wi_hbm, wft_hbm, wr_hbm, wq_hbm, tw_in_hbm, tw_az_hbm, rate, shift, filt, taps,
    out,
    xb, ub, cb, eb, db, fb, lb, pb, twb, mb, c2b, chirp,
    spectrum, wf, wi, wft, wr, wq, tw_in, tw_az, sem_in,
    sem_tw, send1, recv1, sendz, recvz, sendy, recvy, sendn, recvn, sendf, recvf, sem_out,
):
    i = lax.axis_index("rng")
    j = lax.axis_index("az")
    r = i * NA + j
    q = j * NR + i

    zc = lax.rem(j, COL)
    xh = lax.div(j, COL)
    xl = lax.rem(i, 2)
    y = lax.div(i, 2)
    x = 2 * xh + xl
    core = lax.rem(j, 2)
    yx = 4 * y + 2 * xl + xh

    def device(block):
        return (lax.div(block, NA), lax.rem(block, NA))

    def in_column(k):
        return lax.rem(zc + k, COL)

    def in_plane(k):
        to_x = lax.rem(x + k, 4)
        to_y = lax.rem(y + k + lax.div(k, 4), 4)
        to_xl, to_xh = lax.rem(to_x, 2), lax.div(to_x, 2)
        return 4 * to_y + 2 * to_xl + to_xh, (2 * to_y + to_xl, COL * to_xh + zc)

    near = (i, j + 1 - 2 * core)
    far = device(lax.rem(r + NDEV + 2 * core - 1, NDEV))
    leaves = jnp.logical_or(zc == 0, zc == COL - 1)

    def turned(n, last, flip):
        return n + flip * (last - 2 * n)

    barrier = pltpu.get_barrier_semaphore()

    def greet(to):
        pl.semaphore_signal(barrier, inc=1, device_id=to, device_id_type=MESH)

    def greet_column(k, _):
        greet((i, COL * xh + in_column(k)))
        return 0

    def greet_plane(k, _):
        greet(in_plane(k)[1])
        return 0

    lax.fori_loop(1, PLANE, greet_plane, 0)
    lax.fori_loop(1, COL, greet_column, 0)
    greet(far)
    pl.semaphore_wait(barrier, PLANE - 1 + COL - 1 + 1)

    for ch in range(CHUNKS):

        def lines(block, ch=ch):
            return pl.ds(pl.multiple_of(block * LINES + ch * CL, CL), CL)

        def send_lines(k, _, ch=ch, lines=lines):
            to = lax.rem(i + k, NR)
            pltpu.make_async_remote_copy(
                src_ref=raw.at[:, lines(to), :],
                dst_ref=xb.at[i, :, pl.ds(ch * CL, CL), :],
                send_sem=send1.at[ch],
                recv_sem=recv1.at[ch],
                device_id=(to, j),
                device_id_type=MESH,
            ).start()
            return 0

        lax.fori_loop(1, NR, send_lines, 0)
        pltpu.make_async_copy(
            raw.at[:, lines(i), :], xb.at[i, :, pl.ds(ch * CL, CL), :], recv1.at[ch]
        ).start()

    tw_copy = pltpu.make_async_copy(tw_out_hbm, twb, sem_tw)
    tw_copy.start()
    loads = [
        pltpu.make_async_copy(source, place, sem_in.at[n])
        for n, (source, place) in enumerate(
            (
                (spectrum_hbm, spectrum), (wft_hbm, wft), (tw_in_hbm, tw_in), (wr_hbm, wr),
                (wq_hbm, wq), (wf_hbm, wf), (tw_az_hbm, tw_az), (wi_hbm, wi),
            )
        )
    ]
    for load in loads:
        load.start()
    loads[0].wait()

    for part in range(2):
        rows = [spectrum[part : part + 1, 128 * n : 128 * n + 128] for n in range(32)]
        tall = jnp.concatenate(rows + [jnp.zeros((96, 128), F32)], axis=0).T
        spread = tall[:32]
        for n in range(1, 4):
            spread = spread + pltpu.roll(tall[32 * n : 32 * n + 32], 32 * n, 1)
        chirp[part] = spread * (1.0 / NRG)

    f1 = lax.broadcasted_iota(jnp.int32, (128, 128), 0)
    f0 = lax.broadcasted_iota(jnp.int32, (128, 128), 1)
    freq = f0 + 128 * f1
    freq = jnp.where(freq >= NAZ // 2, freq - NAZ, freq)
    c = freq.astype(F32) * (1.0 / NAZ)
    c2b[...] = c * c

    def phases(b, _):
        cosine, sine = half_turns(rate[b] * c2b[...])
        pb[b, 0] = cosine * (1.0 / NAZ)
        pb[b, 1] = sine * (1.0 / NAZ)
        return 0

    lax.fori_loop(0, BINS, phases, 0)

    def first_two(ch):
        chunk = xb.at[:, :, pl.ds(ch * CL, CL), :]
        pltpu.make_async_copy(chunk, chunk, recv1.at[ch]).wait()

        def first(t, _, ch=ch):
            rows = pl.ds(pl.multiple_of(ch * CL + t * 8, 8), 8)

            def load(n):
                lanes = pl.ds(128 * (n % 4), 128)
                return (xb[n // 4, 0, rows, lanes], xb[n // 4, 1, rows, lanes])

            res = dft32(load, -1.0)
            for k in range(32):
                lanes = pl.ds(128 * (k % 4), 128)
                tr, ti = tw_in[0, k], tw_in[1, k]
                xr, xi = res[k]
                xb[k // 4, 0, rows, lanes] = xr * tr - xi * ti
                xb[k // 4, 1, rows, lanes] = xr * ti + xi * tr
            return 0

        lax.fori_loop(0, CL // 8, first, 0)

        def second(blk, _, ch=ch):
            rows = pl.ds(ch * CL, CL)
            parts = []
            for m in range(8):
                s = blk * 2 + m // 4
                lanes = pl.ds(128 * (m % 4), 128)
                parts.append(
                    jnp.concatenate([xb[s, 0, rows, lanes], xb[s, 1, rows, lanes]], axis=1)
                )
            y = dot_nn(three(jnp.concatenate(parts, axis=0), 1), wft[...])
            for m in range(8):
                s = blk * 2 + m // 4
                lanes = pl.ds(128 * (m % 4), 128)
                yr = y[m * CL : m * CL + CL, :128]
                yi = y[m * CL : m * CL + CL, 128:]
                hr = chirp[0, pl.ds(blk * 8 + m, 1), :]
                hi = chirp[1, pl.ds(blk * 8 + m, 1), :]
                xb[s, 0, rows, lanes] = yr * hr - yi * hi
                xb[s, 1, rows, lanes] = yr * hi + yi * hr
            return 0

        lax.fori_loop(0, 4, second, 0)

    def third(half):
        lines = pl.ds(half * HL, HL)

        def step(n, _):
            parts = []
            for m in range(4):
                lanes = pl.ds(128 * m, 128)
                parts.append(
                    jnp.concatenate([xb[n, 0, lines, lanes], xb[n, 1, lines, lanes]], axis=1)
                )
            y = dot_nt(wr[...], three(jnp.concatenate(parts, axis=0), 1))
            for h in range(2):
                z = y[:, 128 * h : 128 * h + 128].reshape(16, 2, 8, 128)
                pair = swap_halves(z[:, 0].reshape(128, 128), z[:, 1].reshape(128, 128))
                for m in range(2):
                    k = n * 4 + 2 * h + m
                    zr, zi = pair[m][:64], pair[m][64:]
                    tr, ti = twb[k, 0], twb[k, 1]
                    row = pl.multiple_of(128 * k, 128)
                    ub[pl.ds(row, 64), :] = zr * tr - zi * ti
                    ub[pl.ds(row + 64, 64), :] = zr * ti + zi * tr
            return 0

        lax.fori_loop(0, NR, step, 0)

    def fourth(half, part):
        quarter = 2 * half + part

        def step(n, _):
            own = lax.rem(r, 4)
            beta = (n + own) - 2 * (
                lax.rem(n, 2) * lax.rem(own, 2) + 2 * lax.div(n, 2) * lax.div(own, 2)
            )
            to_core = lax.rem(beta, 2)
            row = pl.multiple_of(8 * (2 * beta + part + to_core - 2 * part * to_core), 8)

            def load(k):
                return (ub[pl.ds(row + 128 * k, 8), :], ub[pl.ds(row + 128 * k + 64, 8), :])

            res = dft32(load, 1.0)
            for a in range(32):
                base = quarter * QROWS + (4 * (a % 2) + beta) * 256 + (a // 2) * 16
                cb[pl.ds(pl.multiple_of(base, 8), 8), :] = res[a][0]
                cb[pl.ds(pl.multiple_of(base + 8, 8), 8), :] = res[a][1]
            for zh in range(2):
                to = 4 * zh + beta
                rows = pl.ds(pl.multiple_of(quarter * QROWS + to * 256, 256), 256)
                place = eb.at[quarter * COL + zc]

                @pl.when(to != zc)
                def _(rows=rows, to=to, place=place):
                    pltpu.make_async_remote_copy(
                        src_ref=cb.at[rows, :],
                        dst_ref=place,
                        send_sem=sendz.at[quarter],
                        recv_sem=recvz.at[quarter],
                        device_id=(i, COL * xh + to),
                        device_id_type=MESH,
                    ).start()

                @pl.when(to == zc)
                def _(rows=rows, place=place):
                    pltpu.make_async_copy(cb.at[rows, :], place, recvz.at[quarter]).start()

            return 0

        lax.fori_loop(0, 4, step, 0)

    def forward(half, part):
        quarter = 2 * half + part
        landed = eb.at[pl.ds(quarter * COL, COL)]
        pltpu.make_async_copy(landed, landed, recvz.at[quarter]).wait()
        place = db.at[pl.ds(quarter * 128 + yx * COL, COL)]

        def send(k, _):
            to, to_device = in_plane(k)
            pltpu.make_async_remote_copy(
                src_ref=landed.at[:, pl.ds(pl.multiple_of(to * 16, 16), 16), :],
                dst_ref=place,
                send_sem=sendy.at[quarter],
                recv_sem=recvy.at[quarter],
                device_id=to_device,
                device_id_type=MESH,
            ).start()
            return 0

        lax.fori_loop(1, PLANE, send, 0)
        pltpu.make_async_copy(
            landed.at[:, pl.ds(pl.multiple_of(yx * 16, 16), 16), :], place, recvy.at[quarter]
        ).start()

    for load in loads[1:]:
        load.wait()
    first_two(0)
    first_two(1)
    tw_copy.wait()
    third(0)
    fourth(0, 0)
    fourth(0, 1)
    first_two(2)
    forward(0, 0)
    first_two(3)
    third(1)
    fourth(1, 0)
    forward(0, 1)
    fourth(1, 1)
    forward(1, 0)
    forward(1, 1)

    def send_near(m):
        row = 2 * turned(m, 15, core)
        pltpu.make_async_remote_copy(
            src_ref=fb.at[pl.ds(BINS + row, 2)],
            dst_ref=fb.at[pl.ds(2 * BINS * core + row, 2)],
            send_sem=sendn,
            recv_sem=recvn,
            device_id=near,
            device_id_type=MESH,
        ).start()

    def send_far(m):
        row = 2 * turned(m, 15, core)
        pltpu.make_async_remote_copy(
            src_ref=fb.at[pl.ds(BINS + row, 2)],
            dst_ref=lb.at[pl.ds(2 * m, 2)],
            send_sem=sendf,
            recv_sem=recvf.at[lax.div(m, 2)],
            device_id=far,
            device_id_type=MESH,
        ).start()

    flat = db.reshape(HALVES * HALVES * QROWS, 128)
    for part in range(HALVES):
        for half in range(HALVES):
            landed = db.at[pl.ds((2 * half + part) * 128, 128)]
            pltpu.make_async_copy(landed, landed, recvy.at[2 * half + part]).wait()

        if part == 1:
            @pl.when(leaves)
            def _():
                def late(m, _):
                    send_far(m)
                    return 0

                lax.fori_loop(0, 8, late, 0)

        def azimuth(m, part=part):
            s = turned(m - 8 * part, 7, core)
            cols = []
            for half in range(HALVES):
                base = (2 * half + part) * QROWS + s
                re = flat[pl.ds(base, 128, stride=16), :]
                im = flat[pl.ds(base + 8, 128, stride=16), :]
                cols.append(jnp.concatenate([re, im], axis=0))
            out_pair = dft_pair(wq, wf, jnp.concatenate(cols, axis=1), tw_az, False, mixed=True)
            row = BINS + 2 * turned(m, 15, core)
            fb[row] = out_pair[:, :128]
            fb[row + 1] = out_pair[:, 128:]

        def azimuth_two(n, _, part=part, azimuth=azimuth):
            m = 8 * part + 2 * n
            azimuth(m)
            azimuth(m + 1)
            for k in range(2):
                send_near(m + k)
                if part == 1:
                    send_far(m + k)
                else:
                    pl.when(jnp.logical_not(leaves))(functools.partial(send_far, m + k))
            return 0

        lax.fori_loop(0, 4, azimuth_two, 0)

    others = fb.at[pl.ds(0, BINS)]
    pltpu.make_async_copy(others, others, recvn).wait()
    outside = jnp.logical_or(r + core == 0, r + core == NDEV)

    def focus(n, mb):
        for m in range(2):
            b = 2 * n + m
            lanes = pl.ds(128 * m, 128)
            for g in range(GROUPS):
                first_row = BINS + b + shift[g, b] - 4
                which = filt[g, b]
                re, im = pl.ds(8 * g, 8), pl.ds(128 + 8 * g, 8)
                sr = si = None
                for t in range(TAPS):
                    w = taps[t, which]
                    vr = fb[first_row + t, re, :] * w
                    vi = fb[first_row + t, im, :] * w
                    sr = vr if sr is None else sr + vr
                    si = vi if si is None else si + vi
                pc, ps = pb[b, 0, re, :], pb[b, 1, re, :]
                mb[re, lanes] = sr * pc + si * ps
                mb[im, lanes] = si * pc - sr * ps
        y = dft_pair(wi, wi, mb[...], tw_az, True)
        for m in range(2):
            b = 2 * n + m
            for c in range(2):
                base = (c * 4 + lax.div(b, 8)) * 1024 + lax.rem(b, 8)
                ub[pl.ds(base, 128, stride=8), :] = y[128 * c : 128 * c + 128, 128 * m : 128 * m + 128]

    for group in range(8):
        rows = lb.at[pl.ds(4 * group, 4)]
        pltpu.make_async_copy(rows, rows, recvf.at[group]).wait()
        for k in range(2):
            m = 2 * group + k
            row = 2 * turned(m, 15, 1 - core) + 2 * BINS * core
            for h in range(2):
                fb[row + h] = jnp.where(outside, 0.0, lb[2 * m + h])
        for k in range(2):
            focus(turned(2 * group + k, 15, 1 - core), mb.at[k])
        if group % 2 == 1:
            eight = turned(group // 2, 3, 1 - core)
            for c in range(2):
                rows = pl.ds(pl.multiple_of((c * 4 + eight) * 1024, 1024), 1024)
                sem = sem_out.at[group - 1 + c]
                pltpu.make_async_copy(ub.at[rows, :], out.at[rows, :], sem).start()

    for ch in range(CHUNKS):
        gone = xb.at[pl.ds(0, NR - 1), :, pl.ds(ch * CL, CL), :]
        pltpu.make_async_copy(gone, gone, send1.at[ch]).wait()
    for quarter in range(4):
        gone = cb.at[pl.ds(0, (COL - 1) * 256), :]
        pltpu.make_async_copy(gone, gone, sendz.at[quarter]).wait()
        gone = eb.at[pl.ds(0, COL), pl.ds(0, (PLANE - 1) * 16), :]
        pltpu.make_async_copy(gone, gone, sendy.at[quarter]).wait()
    gone = fb.at[pl.ds(BINS, BINS)]
    pltpu.make_async_copy(gone, gone, sendn).wait()
    pltpu.make_async_copy(gone, gone, sendf).wait()
    for n in range(8):
        rows = pl.ds(1024 * n, 1024)
        pltpu.make_async_copy(ub.at[rows, :], out.at[rows, :], sem_out.at[n]).wait()


def local(raw_echo, chirp_spectrum, azimuth_rate, shift_table, filter_index, tap_table):
    wf, wi, wft, wr, wq, tw_in, tw_out, tw_az = tables()
    smem = pl.BlockSpec(memory_space=pltpu.SMEM)
    hbm = pl.BlockSpec(memory_space=pl.ANY)
    dma = pltpu.SemaphoreType.DMA
    image = pl.pallas_call(
        kernel,
        out_shape=jax.ShapeDtypeStruct((8192, 128), F32),
        in_specs=[hbm] * 10 + [smem] * 4,
        out_specs=hbm,
        scratch_shapes=[
            pltpu.VMEM((NR, 2, LINES, 512), F32),
            pltpu.VMEM((8192, 128), F32),
            pltpu.VMEM((4 * QROWS, 128), F32),
            pltpu.VMEM((4 * COL, 256, 128), F32),
            pltpu.VMEM((512, 16, 128), F32),
            pltpu.VMEM((3 * BINS, 256, 128), F32),
            pltpu.VMEM((BINS, 256, 128), F32),
            pltpu.VMEM((BINS, 2, 128, 128), F32),
            pltpu.VMEM((32, 2, 64, 128), F32),
            pltpu.VMEM((2, 256, 256), F32),
            pltpu.VMEM((128, 128), F32),
            pltpu.VMEM((2, 32, 128), F32),
            pltpu.VMEM((2, NRG), F32),
            pltpu.VMEM((256, 768), BF16),
            pltpu.VMEM((256, 768), BF16),
            pltpu.VMEM((768, 256), BF16),
            pltpu.VMEM((256, 768), BF16),
            pltpu.VMEM((256, 768), BF16),
            pltpu.VMEM((2, 32, 8, 128), F32),
            pltpu.VMEM((2, 128, 128), F32),
            dma((8,)),
            dma,
            dma((CHUNKS,)),
            dma((CHUNKS,)),
            dma((4,)),
            dma((4,)),
            dma((4,)),
            dma((4,)),
            dma,
            dma,
            dma,
            dma((8,)),
            dma((8,)),
        ],
        compiler_params=pltpu.CompilerParams(
            collective_id=0, has_side_effects=True, vmem_limit_bytes=60 * 1024 * 1024
        ),
        cost_estimate=pl.CostEstimate(
            flops=10_000_000_000, bytes_accessed=16 * 1024 * 1024, transcendentals=0
        ),
        name="focus_slab",
    )(
        raw_echo, chirp_spectrum, tw_out, wf, wi, wft, wr, wq, tw_in, tw_az,
        azimuth_rate, shift_table, filter_index, tap_table.T,
    )
    image = image.reshape(2, 4, 128, 8, 128).transpose(0, 1, 3, 2, 4)
    return image.reshape(2, BINS, NAZ)


def solution(mesh):
    return jax.shard_map(
        local,
        mesh=mesh,
        in_specs=(
            P(None, "az", "rng"),
            P(),
            P(("rng", "az")),
            P(None, ("rng", "az")),
            P(None, ("rng", "az")),
            P(),
        ),
        out_specs=P(None, ("rng", "az"), None),
        check_vma=False,
    )
```
